32 devices in a mesh: tm: 4 (over y, x), space: 8 (over z, core).
Axes of the slice: x: 2, y: 2, z: 4, core: 2. Of those that a mesh axis runs over, the one named last changes fastest.
Arguments:
- start_values: float32 [4, 64, 128, 128], P('tm', 'space'), may hold values from -6 to 6
- regions: int32 [64, 128, 128], P('space'), may hold values from 0 to 3
- resistivity: float32 [4], replicated, may hold values from 0.1 to 1
Outputs:
- slice_ends: float32 [4, 64, 128, 128], P('tm', 'space')
The draws below stay inside these ranges and needn't reach their ends.
All inputs are finite; a program needn't handle non-finite values.
Results may differ from the reference program's by a relative error of at most 0.0003.
Values sent between devices are 32-bit elements; how exact they have to be, the bound alone decides.
A program may use at most 64 MiB of HBM per device.

```python
import math
import jax
import jax.numpy as jnp
from jax import lax

NY = 128
NZ = 128
STEPS = 8
REGIONS = 4
SLICES = 4
NX = 64


def plant(drawn, own_key, least, top_value):
    shape = drawn.shape
    spot = [jax.random.randint(jax.random.fold_in(own_key, axis), (), 0, shape[axis]) for axis in range(len(shape))]
    drawn = drawn.at[tuple(spot)].set(least)
    longest = shape.index(max(shape))
    spot[longest] = (spot[longest] + 1) % shape[longest]
    return drawn.at[tuple(spot)].set(top_value)


def levels(rng, dims, cuts, smallest, top_value):
    def one(axis_at, blocks):
        steps = jax.random.uniform(jax.random.fold_in(jax.random.fold_in(rng, 6), axis_at), (blocks,), jnp.float32, smallest / len(cuts), top_value / len(cuts))
        return jnp.repeat(jnp.exp(steps), dims[axis_at] // blocks).reshape((-1,) + (1,) * (len(dims) - axis_at - 1))

    loudness = one(*cuts[0])
    for cut in cuts[1:]:
        loudness = loudness * one(*cut)
    return loudness


def noise(rng, extent, spread, limit, split=(), kind=jnp.bfloat16):
    drawn = spread * jax.random.normal(rng, extent, jnp.float32)
    if split:
        drawn = drawn * levels(rng, extent, split, -0.22, 0.18)
    return jnp.clip(drawn, -limit, limit).astype(kind)


def setup_inputs(seed: int = 0) -> dict:
    arg_keys = jax.random.split(jax.random.key(seed), 4)
    return {
        "start_values": noise(arg_keys[0], (SLICES, NX, NY, NZ), 1.0, 6.0, ((0, 4), (1, 8)), jnp.float32),
        "regions": plant(jax.random.randint(arg_keys[1], (NX, NY, NZ), 0, REGIONS), jax.random.fold_in(arg_keys[1], 1), 0, REGIONS - 1).astype(jnp.int32),
        "resistivity": jnp.clip(jnp.exp(jax.random.uniform(arg_keys[2], (REGIONS,), jnp.float32, math.log(0.1), math.log(1.0))), 0.1, 1.0),
    }


fine_step = 0.008


def lookup(regions, resistivity):
    result = jnp.zeros(regions.shape, jnp.float32)
    for region in range(resistivity.shape[0]):
        result = result + jnp.where(regions == region, resistivity[region], jnp.float32(0.0))
    return result


def conduct(field_pad, resist_pad, step_size):
    squared = field_pad * field_pad
    coeff = resist_pad * (1.0 + squared / (1.0 + squared))
    center = field_pad[1:-1, 1:-1, 1:-1]
    coeff_mid = coeff[1:-1, 1:-1, 1:-1]
    flux_sum = jnp.zeros_like(center)
    for axis_dim in range(3):
        for offset in (0, 2):
            index_list = [slice(1, -1)] * 3
            index_list[axis_dim] = slice(offset, offset + center.shape[axis_dim])
            neighbor = field_pad[tuple(index_list)]
            neighbor_coeff = coeff[tuple(index_list)]
            flux_sum = flux_sum + 0.5 * (coeff_mid + neighbor_coeff) * (neighbor - center)
    return center + step_size * flux_sum


def reference(start_values, regions, resistivity):
    resist_pad = jnp.pad(lookup(regions, resistivity), 1)
    coarse_step = fine_step * STEPS

    def relax(pair):
        start, slot = pair
        field = start
        for repeat in range(STEPS):
            field = conduct(jnp.pad(field, 1), resist_pad, fine_step)
        guess = conduct(jnp.pad(start, 1), resist_pad, coarse_step)
        return jnp.where(slot == 0, field, field - guess)

    sent = lax.map(relax, (start_values, jnp.arange(SLICES, dtype=jnp.int32)))

    def chain_turn(carry, source):
        advanced = conduct(jnp.pad(carry, 1), resist_pad, coarse_step) + source
        return advanced, advanced

    final, later = lax.scan(chain_turn, sent[0], sent[1:])
    return jnp.concatenate([sent[:1], later], 0)
```

```python
import functools

import jax
import jax.numpy as jnp
from jax import lax
from jax.experimental import pallas as pl
from jax.experimental.pallas import tpu as pltpu
from jax.sharding import PartitionSpec as P

STEPS = 8
fine_step = 0.008
WIDTH = 2
PAD = 8
CHUNK = 32
STRIP = 16
MESH = pl.DeviceIdType.MESH


def coefficient(field, scaled):
    denominator = 1.0 + field * field
    estimate = pl.reciprocal(denominator, approx=True)
    inverse = estimate * (2.0 - denominator * estimate)
    return scaled * (2.0 - inverse)


def sweep(field_at, coeff_at, planes, row, count, emit):
    rows = pl.ds(row, count)
    lane = lax.broadcasted_iota(jnp.int32, (count, field_at.shape[-1]), 1)
    lanes = field_at.shape[-1]
    is_first, is_last = lane == 0, lane == lanes - 1
    low = planes.start
    before, here = field_at[low - 1, rows, :], field_at[low, rows, :]
    k_before, k_here = coeff_at[low - 1, rows, :], coeff_at[low, rows, :]
    flux_before = (k_before + k_here) * (here - before)
    for plane in planes:
        after, k_after = field_at[plane + 1, rows, :], coeff_at[plane + 1, rows, :]
        flux = (k_here + k_after) * (after - here)
        total = flux - flux_before
        for shift in (-1, 1):
            near = pl.ds(row + shift, count)
            total += (k_here + coeff_at[plane, near, :]) * (field_at[plane, near, :] - here)
        right = jnp.where(is_last, 0.0, pltpu.roll(here, lanes - 1, 1))
        k_right = jnp.where(is_last, 0.0, pltpu.roll(k_here, lanes - 1, 1))
        across = (k_here + k_right) * (right - here)
        total += across - jnp.where(is_first, k_here * here, pltpu.roll(across, 1, 1))
        emit(plane, here, total)
        here, k_here, flux_before = after, k_after, flux


def kernel(
    slices, blocks, start, regions, resistivity, out,
    field, coeff, scaled, halo, guess, relay, relay_coeff,
    halo_send, halo_recv, scaled_send, scaled_recv, relay_send, relay_recv, rim_send, rim_recv,
):
    count, height, lanes = start.shape
    low, high = WIDTH, WIDTH + count
    me_t, me_s = lax.axis_index("tm"), lax.axis_index("space")
    has_low, has_high = me_s > 0, me_s < blocks - 1
    has_prev, has_next = me_t > 0, me_t < slices - 1
    below, above = (me_t, me_s - 1), (me_t, me_s + 1)
    previous, following = (me_t - 1, me_s), (me_t + 1, me_s)
    sides = ((0, has_low, below), (1, has_high, above))

    def chunks(body, size=CHUNK):
        def turn(index, _):
            body(pl.multiple_of(index * size, size))
            return 0

        lax.fori_loop(0, height // size, turn, 0)

    for buffer in (field.at[0], field.at[1], coeff.at[0], coeff.at[1], relay, relay_coeff):
        edge = jnp.zeros((buffer.shape[0], PAD, lanes), jnp.float32)
        buffer[:, pl.ds(0, PAD), :] = edge
        buffer[:, pl.ds(PAD + height, PAD), :] = edge
    for side, present, _ in sides:
        @pl.when(jnp.logical_not(present))
        def _():
            halo[:, side] = jnp.zeros((2, WIDTH, height, lanes), jnp.float32)
            scaled[pl.ds(high * side, WIDTH)] = jnp.zeros((WIDTH, height, lanes), jnp.float32)
            relay[(count + 1) * side, pl.ds(PAD, height), :] = jnp.zeros((height, lanes), jnp.float32)

    barrier = pltpu.get_barrier_semaphore()
    partners = ((has_low, below), (has_high, above), (has_prev, previous), (has_next, following))
    for present, target in partners:
        @pl.when(present)
        def _():
            pl.semaphore_signal(barrier, inc=1, device_id=target, device_id_type=MESH)
    pl.semaphore_wait(barrier, sum(jnp.where(present, 1, 0) for present, _ in partners))

    def remote(source, target, send_sem, recv_sem, device):
        return pltpu.make_async_remote_copy(
            src_ref=source, dst_ref=target, send_sem=send_sem, recv_sem=recv_sem,
            device_id=device, device_id_type=MESH,
        )

    def halo_copy(side, device, slot, source):
        return remote(
            source.at[pl.ds((count - WIDTH) * side, WIDTH)], halo.at[slot, 1 - side],
            halo_send.at[slot, side], halo_recv.at[slot, 1 - side], device,
        )

    def scaled_copy(side, device):
        return remote(
            scaled.at[pl.ds(low + (count - WIDTH) * side, WIDTH)],
            scaled.at[pl.ds(high * (1 - side), WIDTH)],
            scaled_send.at[side], scaled_recv.at[1 - side], device,
        )

    inner = field.at[0, pl.ds(low, count), pl.ds(PAD, height), :]

    for side, present, device in sides:
        @pl.when(present)
        def _():
            halo_copy(side, device, 0, start).start()

    def lookup(plane, rows):
        region = regions[plane, rows, :]
        value = jnp.zeros(region.shape, jnp.float32)
        for index in range(resistivity.shape[0]):
            value = jnp.where(region == index, resistivity[index] * (0.5 * fine_step), value)
        return value

    order = list(range(WIDTH)) + list(range(count - WIDTH, count))

    def outer_scaled(row):
        for plane in order:
            scaled[low + plane, pl.ds(row, CHUNK), :] = lookup(plane, pl.ds(row, CHUNK))

    chunks(outer_scaled)
    for side, present, device in sides:
        @pl.when(present)
        def _():
            scaled_copy(side, device).start()

    def prepare(row):
        rows, padded = pl.ds(row, CHUNK), pl.ds(row + PAD, CHUNK)
        for plane in range(count):
            value = start[plane, rows, :]
            if plane in order:
                factor = scaled[low + plane, rows, :]
            else:
                factor = lookup(plane, rows)
                scaled[low + plane, rows, :] = factor
            field[0, low + plane, padded, :] = value
            coeff[0, low + plane, padded, :] = coefficient(value, factor)

    chunks(prepare)

    coarse = jnp.float32(STEPS)
    subtract = jnp.where(has_prev, 1.0, 0.0).astype(jnp.float32)
    keep = (jnp.where(has_low, 1.0, 0.0).astype(jnp.float32), jnp.where(has_high, 1.0, 0.0).astype(jnp.float32))

    def fine(step, now, planes):
        later = 1 - now
        first, last = step == 0, step == STEPS - 1

        def body(row):
            def emit(plane, value, increment):
                rows, padded = pl.ds(row, CHUNK), pl.ds(row + PAD, CHUNK)
                own = low <= plane < high
                stepped = value + increment
                if first and own:
                    guess[plane - low, rows, :] = subtract * (value + coarse * increment)
                if last:
                    out[plane - low, rows, :] = stepped - guess[plane - low, rows, :]
                    return
                if not own:
                    stepped = stepped * keep[0 if plane < low else 1]
                field[later, plane, padded, :] = stepped
                coeff[later, plane, padded, :] = coefficient(stepped, scaled[plane, rows, :])

            sweep(field.at[now], coeff.at[now], planes, row + PAD, CHUNK, emit)

        chunks(body)

    rounds = STEPS // WIDTH
    for turn in range(rounds):
        slot = turn % 2
        source = start if turn == 0 else inner
        for inside in range(WIDTH):
            fine(turn * WIDTH + inside, inside % 2, range(low + inside + 1, high - inside - 1))
        for side, present, device in sides:
            @pl.when(present)
            def _():
                copy = halo_copy(side, device, slot, source)
                copy.wait_send()
                if turn == 0:
                    scaled_copy(side, device).wait_send()
                    scaled_copy(1 - side, device).wait_recv()
                halo_copy(1 - side, device, slot, source).wait_recv()

            def place(row, side=side):
                rows, padded = pl.ds(row, CHUNK), pl.ds(row + PAD, CHUNK)
                for plane in range(WIDTH):
                    at = high * side + plane
                    value = halo[slot, side, plane, rows, :]
                    field[0, at, padded, :] = value
                    coeff[0, at, padded, :] = coefficient(value, scaled[at, rows, :])

            chunks(place)
            for inside in range(WIDTH):
                reach = WIDTH - 1 - inside
                if side == 0:
                    planes = range(low - reach, low + inside + 1)
                else:
                    planes = range(high - inside - 1, high + reach)
                fine(turn * WIDTH + inside, inside % 2, planes)
            if turn < rounds - 1:
                @pl.when(present)
                def _():
                    halo_copy(side, device, 1 - slot, inner).start()

    strips = height // STRIP

    def strip_rows(strip, offset):
        return pl.ds(pl.multiple_of(strip * STRIP + offset, STRIP if offset % STRIP == 0 else 8), STRIP)

    def relay_copy(strip, device):
        return remote(
            out.at[:, strip_rows(strip, 0), :],
            relay.at[pl.ds(1, count), strip_rows(strip, PAD), :],
            relay_send.at[strip], relay_recv.at[strip], device,
        )

    def rim_copy(side, strip, device):
        rows = strip_rows(strip, PAD)
        return remote(
            relay.at[1 + (count - 1) * side, rows, :],
            relay.at[(count + 1) * (1 - side), rows, :],
            rim_send.at[side, strip], rim_recv.at[1 - side, strip], device,
        )

    @pl.when(jnp.logical_not(has_prev))
    def _():
        def send(strip, _):
            relay_copy(strip, following).start()
            return 0

        lax.fori_loop(0, strips, send, 0)

    @pl.when(has_prev)
    def _():
        def arrive(strip):
            relay_copy(strip, previous).wait_recv()
            for side, present, device in sides:
                @pl.when(present)
                def _():
                    rim_copy(side, strip, device).start()
            rows, padded = strip_rows(strip, 0), strip_rows(strip, PAD)
            for plane in range(count):
                relay_coeff[1 + plane, padded, :] = coefficient(
                    relay[1 + plane, padded, :], scaled[low + plane, rows, :]
                )

        def advance(strip):
            rows, padded = strip_rows(strip, 0), strip_rows(strip, PAD)
            for side, present, device in sides:
                @pl.when(present)
                def _():
                    rim_copy(1 - side, strip, device).wait_recv()
                at = (count + 1) * side
                relay_coeff[at, padded, :] = coefficient(
                    relay[at, padded, :], scaled[low - 1 + at, rows, :]
                )

            def emit(plane, value, increment):
                out[plane - 1, rows, :] = out[plane - 1, rows, :] + (value + coarse * increment)

            sweep(relay, relay_coeff, range(1, count + 1), padded.start, STRIP, emit)

            @pl.when(has_next)
            def _():
                relay_copy(strip, following).start()

        arrive(0)

        def turn(strip, _):
            arrive(strip)
            advance(strip - 1)
            return 0

        lax.fori_loop(1, strips, turn, 0)
        advance(strips - 1)

        def finish(strip, _):
            for side, present, device in sides:
                @pl.when(present)
                def _():
                    rim_copy(side, strip, device).wait_send()
            return 0

        lax.fori_loop(0, strips, finish, 0)

    @pl.when(has_next)
    def _():
        def finish(strip, _):
            relay_copy(strip, following).wait_send()
            return 0

        lax.fori_loop(0, strips, finish, 0)


def per_device(slices, blocks, start_values, regions, resistivity):
    start = start_values[0]
    count, height, lanes = start.shape
    tall, deep = height + 2 * PAD, count + 2 * WIDTH
    strips = height // STRIP
    dma, vmem = pltpu.SemaphoreType.DMA, pltpu.VMEM
    f32 = jnp.float32
    result = pl.pallas_call(
        functools.partial(kernel, slices, blocks),
        out_shape=jax.ShapeDtypeStruct(start.shape, f32),
        in_specs=[
            pl.BlockSpec(memory_space=pltpu.VMEM),
            pl.BlockSpec(memory_space=pltpu.VMEM),
            pl.BlockSpec(memory_space=pltpu.SMEM),
        ],
        out_specs=pl.BlockSpec(memory_space=pltpu.VMEM),
        scratch_shapes=[
            vmem((2, deep, tall, lanes), f32),
            vmem((2, deep, tall, lanes), f32),
            vmem((deep, height, lanes), f32),
            vmem((2, 2, WIDTH, height, lanes), f32),
            vmem(start.shape, f32),
            vmem((count + 2, tall, lanes), f32),
            vmem((count + 2, tall, lanes), f32),
            dma((2, 2)), dma((2, 2)), dma((2,)), dma((2,)),
            dma((strips,)), dma((strips,)), dma((2, strips)), dma((2, strips)),
        ],
        compiler_params=pltpu.CompilerParams(
            collective_id=0, has_side_effects=True, vmem_limit_bytes=32 * 2**20
        ),
        cost_estimate=pl.CostEstimate(flops=start.size * 400, bytes_accessed=start.size * 12, transcendentals=0),
    )(start, regions, resistivity)
    return result[None]


def solution(mesh):
    in_specs = (P("tm", "space", None, None), P("space", None, None), P())
    out_specs = P("tm", "space", None, None)
    return jax.shard_map(
        functools.partial(per_device, mesh.shape["tm"], mesh.shape["space"]),
        mesh=mesh, in_specs=in_specs, out_specs=out_specs, check_vma=False,
    )
```

```python
import functools

import jax
import jax.numpy as jnp
from jax import lax
from jax.experimental import pallas as pl
from jax.experimental.pallas import tpu as pltpu
from jax.sharding import PartitionSpec as P

STEPS = 8
fine_step = 0.008
WIDTH = 2
PAD = 8
CHUNK = 32
STRIP = 8
LAG = 2
HELD = 2
MESH = pl.DeviceIdType.MESH


def coefficient(field, scaled):
    denominator = 1.0 + field * field
    estimate = pl.reciprocal(denominator, approx=True)
    inverse = estimate * (2.0 - denominator * estimate)
    return scaled * (2.0 - inverse)


def sweep(field_at, coeff_at, planes, row, count, emit):
    rows = pl.ds(row, count)
    lane = lax.broadcasted_iota(jnp.int32, (count, field_at.shape[-1]), 1)
    lanes = field_at.shape[-1]
    is_first, is_last = lane == 0, lane == lanes - 1
    low = planes.start
    before, here = field_at[low - 1, rows, :], field_at[low, rows, :]
    k_before, k_here = coeff_at[low - 1, rows, :], coeff_at[low, rows, :]
    flux_before = (k_before + k_here) * (here - before)
    held = []
    for plane in planes:
        after, k_after = field_at[plane + 1, rows, :], coeff_at[plane + 1, rows, :]
        flux = (k_here + k_after) * (after - here)
        total = flux - flux_before
        for shift in (-1, 1):
            near = pl.ds(row + shift, count)
            total += (k_here + coeff_at[plane, near, :]) * (field_at[plane, near, :] - here)
        right = jnp.where(is_last, 0.0, pltpu.roll(here, lanes - 1, 1))
        k_right = jnp.where(is_last, 0.0, pltpu.roll(k_here, lanes - 1, 1))
        across = (k_here + k_right) * (right - here)
        total += across - jnp.where(is_first, k_here * here, pltpu.roll(across, 1, 1))
        held.append(emit(plane, here, total))
        if len(held) > HELD:
            held.pop(0)()
        here, k_here, flux_before = after, k_after, flux
    for store in held:
        store()


def kernel(
    slices, blocks, start_hbm, regions_hbm, resistivity_hbm, out,
    start, regions, resistivity, field_even, field_odd, coeff_even, coeff_odd,
    scaled, halo, guess, relay, relay_coeff, input_sem,
    halo_send, halo_recv, scaled_send, scaled_recv, relay_send, relay_recv, rim_send, rim_recv,
):
    count, height, lanes = start.shape
    field, coeff = (field_even, field_odd), (coeff_even, coeff_odd)
    inputs = [
        pltpu.make_async_copy(source, target, input_sem.at[index])
        for index, (source, target) in enumerate(
            ((resistivity_hbm, resistivity), (regions_hbm, regions), (start_hbm, start))
        )
    ]
    for copy in inputs:
        copy.start()
    low, high = WIDTH, WIDTH + count
    me_t, me_s = lax.axis_index("tm"), lax.axis_index("space")
    has_low, has_high = me_s > 0, me_s < blocks - 1
    has_prev, has_next = me_t > 0, me_t < slices - 1
    below, above = (me_t, me_s - 1), (me_t, me_s + 1)
    previous, following = (me_t - 1, me_s), (me_t + 1, me_s)
    sides = ((0, has_low, below), (1, has_high, above))

    def chunks(body, size=CHUNK):
        def turn(index, _):
            body(pl.multiple_of(index * size, size))
            return 0

        lax.fori_loop(0, height // size, turn, 0)

    for buffer in (*field, *coeff, relay, relay_coeff):
        edge = jnp.zeros((buffer.shape[0], PAD, lanes), jnp.float32)
        buffer[:, pl.ds(0, PAD), :] = edge
        buffer[:, pl.ds(PAD + height, PAD), :] = edge
    for side, present, _ in sides:
        @pl.when(jnp.logical_not(present))
        def _():
            halo[:, side] = jnp.zeros((2, WIDTH, height, lanes), jnp.float32)
            scaled[pl.ds(high * side, WIDTH)] = jnp.zeros((WIDTH, height, lanes), jnp.float32)
            relay[(count + 1) * side, pl.ds(PAD, height), :] = jnp.zeros((height, lanes), jnp.float32)

    barrier = pltpu.get_barrier_semaphore()
    partners = ((has_low, below), (has_high, above), (has_prev, previous), (has_next, following))
    for present, target in partners:
        @pl.when(present)
        def _():
            pl.semaphore_signal(barrier, inc=1, device_id=target, device_id_type=MESH)
    pl.semaphore_wait(barrier, sum(jnp.where(present, 1, 0) for present, _ in partners))

    def remote(source, target, send_sem, recv_sem, device):
        return pltpu.make_async_remote_copy(
            src_ref=source, dst_ref=target, send_sem=send_sem, recv_sem=recv_sem,
            device_id=device, device_id_type=MESH,
        )

    def halo_copy(side, device, slot, source):
        return remote(
            source.at[pl.ds((count - WIDTH) * side, WIDTH)], halo.at[slot, 1 - side],
            halo_send.at[slot, side], halo_recv.at[slot, 1 - side], device,
        )

    def scaled_copy(side, device):
        return remote(
            scaled.at[pl.ds(low + (count - WIDTH) * side, WIDTH)],
            scaled.at[pl.ds(high * (1 - side), WIDTH)],
            scaled_send.at[side], scaled_recv.at[1 - side], device,
        )

    inner = field_even.at[pl.ds(low, count), pl.ds(PAD, height), :]

    for side, present, device in sides:
        @pl.when(present)
        def _():
            halo_copy(side, device, 0, start_hbm).start()

    def lookup(plane, rows):
        region = regions[plane, rows, :]
        value = jnp.zeros(region.shape, jnp.float32)
        for index in range(resistivity.shape[0]):
            value = jnp.where(region == index, resistivity[index] * (0.5 * fine_step), value)
        return value

    order = list(range(WIDTH)) + list(range(count - WIDTH, count))

    def outer_scaled(row):
        for plane in order:
            scaled[low + plane, pl.ds(row, CHUNK), :] = lookup(plane, pl.ds(row, CHUNK))

    inputs[0].wait()
    inputs[1].wait()
    chunks(outer_scaled)
    for side, present, device in sides:
        @pl.when(present)
        def _():
            scaled_copy(side, device).start()

    def prepare(row):
        rows, padded = pl.ds(row, CHUNK), pl.ds(row + PAD, CHUNK)
        for plane in range(count):
            value = start[plane, rows, :]
            if plane in order:
                factor = scaled[low + plane, rows, :]
            else:
                factor = lookup(plane, rows)
                scaled[low + plane, rows, :] = factor
            field_even[low + plane, padded, :] = value
            coeff_even[low + plane, padded, :] = coefficient(value, factor)

    inputs[2].wait()
    chunks(prepare)

    coarse = jnp.float32(STEPS)
    subtract = jnp.where(has_prev, 1.0, 0.0).astype(jnp.float32)
    keep = (jnp.where(has_low, 1.0, 0.0).astype(jnp.float32), jnp.where(has_high, 1.0, 0.0).astype(jnp.float32))

    def fine(step, now, planes):
        later = 1 - now
        first, last = step == 0, step == STEPS - 1

        def body(row):
            def emit(plane, value, increment):
                rows, padded = pl.ds(row, CHUNK), pl.ds(row + PAD, CHUNK)
                own = low <= plane < high
                stepped = value + increment
                if last:
                    result = stepped - guess[plane - low, rows, :]

                    def store_last():
                        out[plane - low, rows, :] = result

                    return store_last
                if not own:
                    stepped = stepped * keep[0 if plane < low else 1]
                factor = coefficient(stepped, scaled[plane, rows, :])

                def store():
                    if first and own:
                        guess[plane - low, rows, :] = subtract * (value + coarse * increment)
                    field[later][plane, padded, :] = stepped
                    coeff[later][plane, padded, :] = factor

                return store

            sweep(field[now], coeff[now], planes, row + PAD, CHUNK, emit)

        chunks(body)

    rounds = STEPS // WIDTH
    for turn in range(rounds):
        slot = turn % 2
        source = start_hbm if turn == 0 else inner
        for inside in range(WIDTH):
            fine(turn * WIDTH + inside, inside % 2, range(low + inside + 1, high - inside - 1))
        for side, present, device in sides:
            @pl.when(present)
            def _():
                copy = halo_copy(side, device, slot, source)
                copy.wait_send()
                if turn == 0:
                    scaled_copy(side, device).wait_send()
                    scaled_copy(1 - side, device).wait_recv()
                halo_copy(1 - side, device, slot, source).wait_recv()

            def place(row, side=side):
                rows, padded = pl.ds(row, CHUNK), pl.ds(row + PAD, CHUNK)
                for plane in range(WIDTH):
                    at = high * side + plane
                    value = halo[slot, side, plane, rows, :]
                    field_even[at, padded, :] = value
                    coeff_even[at, padded, :] = coefficient(value, scaled[at, rows, :])

            chunks(place)
            for inside in range(WIDTH):
                reach = WIDTH - 1 - inside
                if side == 0:
                    planes = range(low - reach, low + inside + 1)
                else:
                    planes = range(high - inside - 1, high + reach)
                fine(turn * WIDTH + inside, inside % 2, planes)
            if turn < rounds - 1:
                @pl.when(present)
                def _():
                    halo_copy(side, device, 1 - slot, inner).start()

    strips = height // STRIP

    def strip_rows(strip, offset):
        return pl.ds(pl.multiple_of(strip * STRIP + offset, STRIP if offset % STRIP == 0 else 8), STRIP)

    def relay_copy(strip, device):
        return remote(
            out.at[:, strip_rows(strip, 0), :],
            relay.at[pl.ds(1, count), strip_rows(strip, PAD), :],
            relay_send.at[strip], relay_recv.at[strip], device,
        )

    def rim_copy(side, strip, device):
        rows = strip_rows(strip, PAD)
        return remote(
            relay.at[1 + (count - 1) * side, rows, :],
            relay.at[(count + 1) * (1 - side), rows, :],
            rim_send.at[side, strip], rim_recv.at[1 - side, strip], device,
        )

    @pl.when(jnp.logical_not(has_prev))
    def _():
        def send(strip, _):
            relay_copy(strip, following).start()
            return 0

        lax.fori_loop(0, strips, send, 0)

    @pl.when(has_prev)
    def _():
        def arrive(strip):
            relay_copy(strip, previous).wait_recv()
            for side, present, device in sides:
                @pl.when(present)
                def _():
                    rim_copy(side, strip, device).start()
            rows, padded = strip_rows(strip, 0), strip_rows(strip, PAD)
            for plane in range(count):
                relay_coeff[1 + plane, padded, :] = coefficient(
                    relay[1 + plane, padded, :], scaled[low + plane, rows, :]
                )

        def advance(strip):
            rows, padded = strip_rows(strip, 0), strip_rows(strip, PAD)
            for side, present, device in sides:
                @pl.when(present)
                def _():
                    rim_copy(1 - side, strip, device).wait_recv()
                at = (count + 1) * side
                relay_coeff[at, padded, :] = coefficient(
                    relay[at, padded, :], scaled[low - 1 + at, rows, :]
                )

            def emit(plane, value, increment):
                result = out[plane - 1, rows, :] + (value + coarse * increment)

                def store():
                    out[plane - 1, rows, :] = result

                return store

            sweep(relay, relay_coeff, range(1, count + 1), padded.start, STRIP, emit)

            @pl.when(has_next)
            def _():
                relay_copy(strip, following).start()

        for strip in range(LAG):
            arrive(strip)

        def turn(strip, _):
            arrive(strip)
            advance(strip - LAG)
            return 0

        lax.fori_loop(LAG, strips, turn, 0)
        for strip in range(strips - LAG, strips):
            advance(strip)

        def finish(strip, _):
            for side, present, device in sides:
                @pl.when(present)
                def _():
                    rim_copy(side, strip, device).wait_send()
            return 0

        lax.fori_loop(0, strips, finish, 0)

    @pl.when(has_next)
    def _():
        def finish(strip, _):
            relay_copy(strip, following).wait_send()
            return 0

        lax.fori_loop(0, strips, finish, 0)


def per_device(slices, blocks, start_values, regions, resistivity):
    start = start_values[0]
    count, height, lanes = start.shape
    tall, deep = height + 2 * PAD, count + 2 * WIDTH
    strips = height // STRIP
    dma, vmem = pltpu.SemaphoreType.DMA, pltpu.VMEM
    f32 = jnp.float32
    result = pl.pallas_call(
        functools.partial(kernel, slices, blocks),
        out_shape=jax.ShapeDtypeStruct(start.shape, f32),
        in_specs=[
            pl.BlockSpec(memory_space=pltpu.HBM),
            pl.BlockSpec(memory_space=pltpu.HBM),
            pl.BlockSpec(memory_space=pltpu.HBM),
        ],
        out_specs=pl.BlockSpec(memory_space=pltpu.VMEM),
        scratch_shapes=[
            vmem(start.shape, f32),
            vmem(regions.shape, regions.dtype),
            pltpu.SMEM(resistivity.shape, f32),
            *[vmem((deep, tall, lanes), f32) for _ in range(4)],
            vmem((deep, height, lanes), f32),
            vmem((2, 2, WIDTH, height, lanes), f32),
            vmem(start.shape, f32),
            vmem((count + 2, tall, lanes), f32),
            vmem((count + 2, tall, lanes), f32),
            dma((3,)), dma((2, 2)), dma((2, 2)), dma((2,)), dma((2,)),
            dma((strips,)), dma((strips,)), dma((2, strips)), dma((2, strips)),
        ],
        compiler_params=pltpu.CompilerParams(
            collective_id=0, has_side_effects=True, vmem_limit_bytes=32 * 2**20
        ),
        cost_estimate=pl.CostEstimate(flops=start.size * 400, bytes_accessed=start.size * 12, transcendentals=0),
    )(start, regions, resistivity)
    return result[None]


def solution(mesh):
    in_specs = (P("tm", "space", None, None), P("space", None, None), P())
    out_specs = P("tm", "space", None, None)
    return jax.shard_map(
        functools.partial(per_device, mesh.shape["tm"], mesh.shape["space"]),
        mesh=mesh, in_specs=in_specs, out_specs=out_specs, check_vma=False,
    )
```

```python
import functools

import jax
import jax.numpy as jnp
from jax import lax
from jax.experimental import pallas as pl
from jax.experimental.pallas import tpu as pltpu
from jax.sharding import PartitionSpec as P

STEPS = 8
fine_step = 0.008
WIDTH = 2
PAD = 8
CHUNK = 32
STRIP = 8
LAG = 2
FLIGHT = 2
HELD = 2
MESH = pl.DeviceIdType.MESH


def coefficient(field, scaled):
    denominator = 1.0 + field * field
    estimate = pl.reciprocal(denominator, approx=True)
    inverse = estimate * (2.0 - denominator * estimate)
    return scaled * (2.0 - inverse)


def sweep(field_at, coeff_at, planes, row, count, emit):
    rows = pl.ds(row, count)
    lane = lax.broadcasted_iota(jnp.int32, (count, field_at.shape[-1]), 1)
    lanes = field_at.shape[-1]
    is_first, is_last = lane == 0, lane == lanes - 1
    low = planes.start
    before, here = field_at[low - 1, rows, :], field_at[low, rows, :]
    k_before, k_here = coeff_at[low - 1, rows, :], coeff_at[low, rows, :]
    flux_before = (k_before + k_here) * (here - before)
    held = []
    for plane in planes:
        after, k_after = field_at[plane + 1, rows, :], coeff_at[plane + 1, rows, :]
        flux = (k_here + k_after) * (after - here)
        total = flux - flux_before
        for shift in (-1, 1):
            near = pl.ds(row + shift, count)
            total += (k_here + coeff_at[plane, near, :]) * (field_at[plane, near, :] - here)
        right = jnp.where(is_last, 0.0, pltpu.roll(here, lanes - 1, 1))
        k_right = jnp.where(is_last, 0.0, pltpu.roll(k_here, lanes - 1, 1))
        across = (k_here + k_right) * (right - here)
        total += across - jnp.where(is_first, k_here * here, pltpu.roll(across, 1, 1))
        held.append(emit(plane, here, total))
        if len(held) > HELD:
            held.pop(0)()
        here, k_here, flux_before = after, k_after, flux
    for store in held:
        store()


def kernel(
    slices, blocks, start_hbm, regions_hbm, resistivity_hbm, out,
    start, regions, resistivity, field_even, field_odd, coeff_even, coeff_odd,
    scaled, halo, guess, relay, relay_coeff, input_sem,
    halo_send, halo_recv, scaled_send, scaled_recv, relay_send, relay_recv, rim_send, rim_recv,
):
    count, height, lanes = start.shape
    field, coeff = (field_even, field_odd), (coeff_even, coeff_odd)
    inputs = [
        pltpu.make_async_copy(source, target, input_sem.at[index])
        for index, (source, target) in enumerate(
            ((resistivity_hbm, resistivity), (regions_hbm, regions), (start_hbm, start))
        )
    ]
    for copy in inputs:
        copy.start()
    low, high = WIDTH, WIDTH + count
    me_t, me_s = lax.axis_index("tm"), lax.axis_index("space")
    has_low, has_high = me_s > 0, me_s < blocks - 1
    has_prev, has_next = me_t > 0, me_t < slices - 1
    below, above = (me_t, me_s - 1), (me_t, me_s + 1)
    previous, following = (me_t - 1, me_s), (me_t + 1, me_s)
    sides = ((0, has_low, below), (1, has_high, above))

    def chunks(body, size=CHUNK):
        def turn(index, _):
            body(pl.multiple_of(index * size, size))
            return 0

        lax.fori_loop(0, height // size, turn, 0)

    for buffer in (*field, *coeff, relay, relay_coeff):
        edge = jnp.zeros((buffer.shape[0], PAD, lanes), jnp.float32)
        buffer[:, pl.ds(0, PAD), :] = edge
        buffer[:, pl.ds(PAD + height, PAD), :] = edge
    for side, present, _ in sides:
        @pl.when(jnp.logical_not(present))
        def _():
            halo[:, side] = jnp.zeros((2, WIDTH, height, lanes), jnp.float32)
            scaled[pl.ds(high * side, WIDTH)] = jnp.zeros((WIDTH, height, lanes), jnp.float32)
            relay[(count + 1) * side, pl.ds(PAD, height), :] = jnp.zeros((height, lanes), jnp.float32)

    barrier = pltpu.get_barrier_semaphore()
    partners = ((has_low, below), (has_high, above), (has_prev, previous), (has_next, following))
    for present, target in partners:
        @pl.when(present)
        def _():
            pl.semaphore_signal(barrier, inc=1, device_id=target, device_id_type=MESH)
    pl.semaphore_wait(barrier, sum(jnp.where(present, 1, 0) for present, _ in partners))

    def remote(source, target, send_sem, recv_sem, device):
        return pltpu.make_async_remote_copy(
            src_ref=source, dst_ref=target, send_sem=send_sem, recv_sem=recv_sem,
            device_id=device, device_id_type=MESH,
        )

    def halo_copy(side, device, slot, source):
        return remote(
            source.at[pl.ds((count - WIDTH) * side, WIDTH)], halo.at[slot, 1 - side],
            halo_send.at[slot, side], halo_recv.at[slot, 1 - side], device,
        )

    def scaled_copy(side, device):
        return remote(
            scaled.at[pl.ds(low + (count - WIDTH) * side, WIDTH)],
            scaled.at[pl.ds(high * (1 - side), WIDTH)],
            scaled_send.at[side], scaled_recv.at[1 - side], device,
        )

    inner = field_even.at[pl.ds(low, count), pl.ds(PAD, height), :]

    for side, present, device in sides:
        @pl.when(present)
        def _():
            halo_copy(side, device, 0, start_hbm).start()

    def lookup(plane, rows):
        region = regions[plane, rows, :]
        value = jnp.zeros(region.shape, jnp.float32)
        for index in range(resistivity.shape[0]):
            value = jnp.where(region == index, resistivity[index] * (0.5 * fine_step), value)
        return value

    order = list(range(WIDTH)) + list(range(count - WIDTH, count))

    def outer_scaled(row):
        for plane in order:
            scaled[low + plane, pl.ds(row, CHUNK), :] = lookup(plane, pl.ds(row, CHUNK))

    inputs[0].wait()
    inputs[1].wait()
    chunks(outer_scaled)
    for side, present, device in sides:
        @pl.when(present)
        def _():
            scaled_copy(side, device).start()

    def prepare(row):
        rows, padded = pl.ds(row, CHUNK), pl.ds(row + PAD, CHUNK)
        for plane in range(count):
            value = start[plane, rows, :]
            if plane in order:
                factor = scaled[low + plane, rows, :]
            else:
                factor = lookup(plane, rows)
                scaled[low + plane, rows, :] = factor
            field_even[low + plane, padded, :] = value
            coeff_even[low + plane, padded, :] = coefficient(value, factor)

    inputs[2].wait()
    chunks(prepare)

    coarse = jnp.float32(STEPS)
    subtract = jnp.where(has_prev, 1.0, 0.0).astype(jnp.float32)
    keep = (jnp.where(has_low, 1.0, 0.0).astype(jnp.float32), jnp.where(has_high, 1.0, 0.0).astype(jnp.float32))

    def fine(step, now, planes):
        later = 1 - now
        first, last = step == 0, step == STEPS - 1

        def body(row):
            def emit(plane, value, increment):
                rows, padded = pl.ds(row, CHUNK), pl.ds(row + PAD, CHUNK)
                own = low <= plane < high
                stepped = value + increment
                if last:
                    result = stepped - guess[plane - low, rows, :]

                    def store_last():
                        out[plane - low, rows, :] = result

                    return store_last
                if not own:
                    stepped = stepped * keep[0 if plane < low else 1]
                factor = coefficient(stepped, scaled[plane, rows, :])

                def store():
                    if first and own:
                        guess[plane - low, rows, :] = subtract * (value + coarse * increment)
                    field[later][plane, padded, :] = stepped
                    coeff[later][plane, padded, :] = factor

                return store

            sweep(field[now], coeff[now], planes, row + PAD, CHUNK, emit)

        chunks(body)

    rounds = STEPS // WIDTH
    for turn in range(rounds):
        slot = turn % 2
        source = start_hbm if turn == 0 else inner
        for inside in range(WIDTH):
            fine(turn * WIDTH + inside, inside % 2, range(low + inside + 1, high - inside - 1))
        for side, present, device in sides:
            @pl.when(present)
            def _():
                copy = halo_copy(side, device, slot, source)
                copy.wait_send()
                if turn == 0:
                    scaled_copy(side, device).wait_send()
                    scaled_copy(1 - side, device).wait_recv()
                halo_copy(1 - side, device, slot, source).wait_recv()

            def place(row, side=side):
                rows, padded = pl.ds(row, CHUNK), pl.ds(row + PAD, CHUNK)
                for plane in range(WIDTH):
                    at = high * side + plane
                    value = halo[slot, side, plane, rows, :]
                    field_even[at, padded, :] = value
                    coeff_even[at, padded, :] = coefficient(value, scaled[at, rows, :])

            chunks(place)
            for inside in range(WIDTH):
                reach = WIDTH - 1 - inside
                if side == 0:
                    planes = range(low - reach, low + inside + 1)
                else:
                    planes = range(high - inside - 1, high + reach)
                fine(turn * WIDTH + inside, inside % 2, planes)
            if turn < rounds - 1:
                @pl.when(present)
                def _():
                    halo_copy(side, device, 1 - slot, inner).start()

    strips = height // STRIP

    def strip_rows(strip, offset):
        return pl.ds(pl.multiple_of(strip * STRIP + offset, STRIP if offset % STRIP == 0 else 8), STRIP)

    def relay_copy(strip, device):
        return remote(
            out.at[:, strip_rows(strip, 0), :],
            relay.at[pl.ds(1, count), strip_rows(strip, PAD), :],
            relay_send.at[strip], relay_recv.at[strip], device,
        )

    def rim_copy(side, strip, device):
        rows = strip_rows(strip, PAD)
        return remote(
            relay.at[1 + (count - 1) * side, rows, :],
            relay.at[(count + 1) * (1 - side), rows, :],
            rim_send.at[side, strip], rim_recv.at[1 - side, strip], device,
        )

    @pl.when(jnp.logical_not(has_prev))
    def _():
        for strip in range(FLIGHT):
            relay_copy(strip, following).start()

        def send(strip, _):
            relay_copy(strip - FLIGHT, following).wait_send()
            relay_copy(strip, following).start()
            return 0

        lax.fori_loop(FLIGHT, strips, send, 0)
        for strip in range(strips - FLIGHT, strips):
            relay_copy(strip, following).wait_send()

    @pl.when(has_prev)
    def _():
        def arrive(strip):
            relay_copy(strip, previous).wait_recv()
            for side, present, device in sides:
                @pl.when(present)
                def _():
                    rim_copy(side, strip, device).start()
            rows, padded = strip_rows(strip, 0), strip_rows(strip, PAD)
            for plane in range(count):
                relay_coeff[1 + plane, padded, :] = coefficient(
                    relay[1 + plane, padded, :], scaled[low + plane, rows, :]
                )

        def advance(strip):
            rows, padded = strip_rows(strip, 0), strip_rows(strip, PAD)
            for side, present, device in sides:
                @pl.when(present)
                def _():
                    rim_copy(1 - side, strip, device).wait_recv()
                at = (count + 1) * side
                relay_coeff[at, padded, :] = coefficient(
                    relay[at, padded, :], scaled[low - 1 + at, rows, :]
                )

            def emit(plane, value, increment):
                result = out[plane - 1, rows, :] + (value + coarse * increment)

                def store():
                    out[plane - 1, rows, :] = result

                return store

            sweep(relay, relay_coeff, range(1, count + 1), padded.start, STRIP, emit)

            @pl.when(has_next)
            def _():
                relay_copy(strip, following).start()

        for strip in range(LAG):
            arrive(strip)

        def turn(strip, _):
            arrive(strip)
            advance(strip - LAG)
            return 0

        lax.fori_loop(LAG, strips, turn, 0)
        for strip in range(strips - LAG, strips):
            advance(strip)

        def finish(strip, _):
            for side, present, device in sides:
                @pl.when(present)
                def _():
                    rim_copy(side, strip, device).wait_send()
            return 0

        lax.fori_loop(0, strips, finish, 0)

    @pl.when(jnp.logical_and(has_prev, has_next))
    def _():
        def finish(strip, _):
            relay_copy(strip, following).wait_send()
            return 0

        lax.fori_loop(0, strips, finish, 0)


def per_device(slices, blocks, start_values, regions, resistivity):
    start = start_values[0]
    count, height, lanes = start.shape
    tall, deep = height + 2 * PAD, count + 2 * WIDTH
    strips = height // STRIP
    dma, vmem = pltpu.SemaphoreType.DMA, pltpu.VMEM
    f32 = jnp.float32
    result = pl.pallas_call(
        functools.partial(kernel, slices, blocks),
        out_shape=jax.ShapeDtypeStruct(start.shape, f32),
        in_specs=[
            pl.BlockSpec(memory_space=pltpu.HBM),
            pl.BlockSpec(memory_space=pltpu.HBM),
            pl.BlockSpec(memory_space=pltpu.HBM),
        ],
        out_specs=pl.BlockSpec(memory_space=pltpu.VMEM),
        scratch_shapes=[
            vmem(start.shape, f32),
            vmem(regions.shape, regions.dtype),
            pltpu.SMEM(resistivity.shape, f32),
            *[vmem((deep, tall, lanes), f32) for _ in range(4)],
            vmem((deep, height, lanes), f32),
            vmem((2, 2, WIDTH, height, lanes), f32),
            vmem(start.shape, f32),
            vmem((count + 2, tall, lanes), f32),
            vmem((count + 2, tall, lanes), f32),
            dma((3,)), dma((2, 2)), dma((2, 2)), dma((2,)), dma((2,)),
            dma((strips,)), dma((strips,)), dma((2, strips)), dma((2, strips)),
        ],
        compiler_params=pltpu.CompilerParams(
            collective_id=0, has_side_effects=True, vmem_limit_bytes=32 * 2**20
        ),
        cost_estimate=pl.CostEstimate(flops=start.size * 400, bytes_accessed=start.size * 12, transcendentals=0),
    )(start, regions, resistivity)
    return result[None]


def solution(mesh):
    in_specs = (P("tm", "space", None, None), P("space", None, None), P())
    out_specs = P("tm", "space", None, None)
    return jax.shard_map(
        functools.partial(per_device, mesh.shape["tm"], mesh.shape["space"]),
        mesh=mesh, in_specs=in_specs, out_specs=out_specs, check_vma=False,
    )
```

```python
import functools

import jax
import jax.numpy as jnp
from jax import lax
from jax.experimental import pallas as pl
from jax.experimental.pallas import tpu as pltpu
from jax.sharding import PartitionSpec as P

STEPS = 8
fine_step = 0.008
WIDTH = 2
PAD = 8
CHUNK = 32
STRIP = 8
LAG = 4
FLIGHT = 4
HELD = 2
MESH = pl.DeviceIdType.MESH


def coefficient(field, scaled):
    denominator = 1.0 + field * field
    estimate = pl.reciprocal(denominator, approx=True)
    inverse = estimate * (2.0 - denominator * estimate)
    return scaled * (2.0 - inverse)


def sweep(field_at, coeff_at, planes, row, count, emit):
    rows = pl.ds(row, count)
    lane = lax.broadcasted_iota(jnp.int32, (count, field_at.shape[-1]), 1)
    lanes = field_at.shape[-1]
    is_first, is_last = lane == 0, lane == lanes - 1
    low = planes.start
    before, here = field_at[low - 1, rows, :], field_at[low, rows, :]
    k_before, k_here = coeff_at[low - 1, rows, :], coeff_at[low, rows, :]
    flux_before = (k_before + k_here) * (here - before)
    held = []
    for plane in planes:
        after, k_after = field_at[plane + 1, rows, :], coeff_at[plane + 1, rows, :]
        flux = (k_here + k_after) * (after - here)
        total = flux - flux_before
        for shift in (-1, 1):
            near = pl.ds(row + shift, count)
            total += (k_here + coeff_at[plane, near, :]) * (field_at[plane, near, :] - here)
        right = jnp.where(is_last, 0.0, pltpu.roll(here, lanes - 1, 1))
        k_right = jnp.where(is_last, 0.0, pltpu.roll(k_here, lanes - 1, 1))
        across = (k_here + k_right) * (right - here)
        total += across - jnp.where(is_first, k_here * here, pltpu.roll(across, 1, 1))
        held.append(emit(plane, here, total))
        if len(held) > HELD:
            held.pop(0)()
        here, k_here, flux_before = after, k_after, flux
    for store in held:
        store()


def kernel(
    slices, blocks, start_hbm, regions_hbm, resistivity_hbm, out,
    start, regions, resistivity, field_even, field_odd, coeff_even, coeff_odd,
    scaled, halo, guess, relay, relay_coeff, input_sem,
    halo_send, halo_recv, scaled_send, scaled_recv, relay_send, relay_recv, rim_send, rim_recv,
):
    count, height, lanes = start.shape
    field, coeff = (field_even, field_odd), (coeff_even, coeff_odd)
    inputs = [
        pltpu.make_async_copy(source, target, input_sem.at[index])
        for index, (source, target) in enumerate(
            ((resistivity_hbm, resistivity), (regions_hbm, regions), (start_hbm, start))
        )
    ]
    for copy in inputs:
        copy.start()
    low, high = WIDTH, WIDTH + count
    me_t, me_s = lax.axis_index("tm"), lax.axis_index("space")
    has_low, has_high = me_s > 0, me_s < blocks - 1
    has_prev, has_next = me_t > 0, me_t < slices - 1
    below, above = (me_t, me_s - 1), (me_t, me_s + 1)
    previous, following = (me_t - 1, me_s), (me_t + 1, me_s)
    sides = ((0, has_low, below), (1, has_high, above))

    def chunks(body, size=CHUNK):
        def turn(index, _):
            body(pl.multiple_of(index * size, size))
            return 0

        lax.fori_loop(0, height // size, turn, 0)

    for buffer in (*field, *coeff, relay, relay_coeff):
        edge = jnp.zeros((buffer.shape[0], PAD, lanes), jnp.float32)
        buffer[:, pl.ds(0, PAD), :] = edge
        buffer[:, pl.ds(PAD + height, PAD), :] = edge
    for side, present, _ in sides:
        @pl.when(jnp.logical_not(present))
        def _():
            halo[:, side] = jnp.zeros((2, WIDTH, height, lanes), jnp.float32)
            scaled[pl.ds(high * side, WIDTH)] = jnp.zeros((WIDTH, height, lanes), jnp.float32)
            relay[(count + 1) * side, pl.ds(PAD, height), :] = jnp.zeros((height, lanes), jnp.float32)

    barrier = pltpu.get_barrier_semaphore()
    partners = ((has_low, below), (has_high, above), (has_prev, previous), (has_next, following))
    for present, target in partners:
        @pl.when(present)
        def _():
            pl.semaphore_signal(barrier, inc=1, device_id=target, device_id_type=MESH)
    pl.semaphore_wait(barrier, sum(jnp.where(present, 1, 0) for present, _ in partners))

    def remote(source, target, send_sem, recv_sem, device):
        return pltpu.make_async_remote_copy(
            src_ref=source, dst_ref=target, send_sem=send_sem, recv_sem=recv_sem,
            device_id=device, device_id_type=MESH,
        )

    def halo_copy(side, device, slot, source):
        return remote(
            source.at[pl.ds((count - WIDTH) * side, WIDTH)], halo.at[slot, 1 - side],
            halo_send.at[slot, side], halo_recv.at[slot, 1 - side], device,
        )

    def scaled_copy(side, device):
        return remote(
            scaled.at[pl.ds(low + (count - WIDTH) * side, WIDTH)],
            scaled.at[pl.ds(high * (1 - side), WIDTH)],
            scaled_send.at[side], scaled_recv.at[1 - side], device,
        )

    inner = field_even.at[pl.ds(low, count), pl.ds(PAD, height), :]

    for side, present, device in sides:
        @pl.when(present)
        def _():
            halo_copy(side, device, 0, start_hbm).start()

    def lookup(plane, rows):
        region = regions[plane, rows, :]
        value = jnp.zeros(region.shape, jnp.float32)
        for index in range(resistivity.shape[0]):
            value = jnp.where(region == index, resistivity[index] * (0.5 * fine_step), value)
        return value

    order = list(range(WIDTH)) + list(range(count - WIDTH, count))

    def outer_scaled(row):
        for plane in order:
            scaled[low + plane, pl.ds(row, CHUNK), :] = lookup(plane, pl.ds(row, CHUNK))

    inputs[0].wait()
    inputs[1].wait()
    chunks(outer_scaled)
    for side, present, device in sides:
        @pl.when(present)
        def _():
            scaled_copy(side, device).start()

    def prepare(row):
        rows, padded = pl.ds(row, CHUNK), pl.ds(row + PAD, CHUNK)
        for plane in range(count):
            value = start[plane, rows, :]
            if plane in order:
                factor = scaled[low + plane, rows, :]
            else:
                factor = lookup(plane, rows)
                scaled[low + plane, rows, :] = factor
            field_even[low + plane, padded, :] = value
            coeff_even[low + plane, padded, :] = coefficient(value, factor)

    inputs[2].wait()
    chunks(prepare)

    coarse = jnp.float32(STEPS)
    subtract = jnp.where(has_prev, 1.0, 0.0).astype(jnp.float32)
    keep = (jnp.where(has_low, 1.0, 0.0).astype(jnp.float32), jnp.where(has_high, 1.0, 0.0).astype(jnp.float32))

    def fine(step, now, planes):
        later = 1 - now
        first, last = step == 0, step == STEPS - 1

        def body(row):
            def emit(plane, value, increment):
                rows, padded = pl.ds(row, CHUNK), pl.ds(row + PAD, CHUNK)
                own = low <= plane < high
                stepped = value + increment
                if last:
                    result = stepped - guess[plane - low, rows, :]

                    def store_last():
                        out[plane - low, rows, :] = result

                    return store_last
                if not own:
                    stepped = stepped * keep[0 if plane < low else 1]
                factor = coefficient(stepped, scaled[plane, rows, :])

                def store():
                    if first and own:
                        guess[plane - low, rows, :] = subtract * (value + coarse * increment)
                    field[later][plane, padded, :] = stepped
                    coeff[later][plane, padded, :] = factor

                return store

            sweep(field[now], coeff[now], planes, row + PAD, CHUNK, emit)

        chunks(body)

    rounds = STEPS // WIDTH
    is_even = lax.rem(me_s, 2) == 0
    for turn in range(rounds):
        slot = turn % 2
        source = start_hbm if turn == 0 else inner
        for inside in range(WIDTH):
            fine(turn * WIDTH + inside, inside % 2, range(low + inside + 1, high - inside - 1))
        def finish_side(side, present, device, turn=turn, slot=slot, source=source):
            @pl.when(present)
            def _():
                copy = halo_copy(side, device, slot, source)
                copy.wait_send()
                if turn == 0:
                    scaled_copy(side, device).wait_send()
                    scaled_copy(1 - side, device).wait_recv()
                halo_copy(1 - side, device, slot, source).wait_recv()

            def place(row, side=side):
                rows, padded = pl.ds(row, CHUNK), pl.ds(row + PAD, CHUNK)
                for plane in range(WIDTH):
                    at = high * side + plane
                    value = halo[slot, side, plane, rows, :]
                    field_even[at, padded, :] = value
                    coeff_even[at, padded, :] = coefficient(value, scaled[at, rows, :])

            chunks(place)
            for inside in range(WIDTH):
                reach = WIDTH - 1 - inside
                if side == 0:
                    planes = range(low - reach, low + inside + 1)
                else:
                    planes = range(high - inside - 1, high + reach)
                fine(turn * WIDTH + inside, inside % 2, planes)
            if turn < rounds - 1:
                @pl.when(present)
                def _():
                    halo_copy(side, device, 1 - slot, inner).start()

        @pl.when(is_even)
        def _():
            for side in reversed(sides):
                finish_side(*side)

        @pl.when(jnp.logical_not(is_even))
        def _():
            for side in sides:
                finish_side(*side)

    strips = height // STRIP

    def strip_rows(strip, offset):
        return pl.ds(pl.multiple_of(strip * STRIP + offset, STRIP if offset % STRIP == 0 else 8), STRIP)

    def relay_copy(strip, device):
        return remote(
            out.at[:, strip_rows(strip, 0), :],
            relay.at[pl.ds(1, count), strip_rows(strip, PAD), :],
            relay_send.at[strip], relay_recv.at[strip], device,
        )

    def rim_copy(side, strip, device):
        rows = strip_rows(strip, PAD)
        return remote(
            relay.at[1 + (count - 1) * side, rows, :],
            relay.at[(count + 1) * (1 - side), rows, :],
            rim_send.at[side, strip], rim_recv.at[1 - side, strip], device,
        )

    @pl.when(jnp.logical_not(has_prev))
    def _():
        for strip in range(FLIGHT):
            relay_copy(strip, following).start()

        def send(strip, _):
            relay_copy(strip - FLIGHT, following).wait_send()
            relay_copy(strip, following).start()
            return 0

        lax.fori_loop(FLIGHT, strips, send, 0)
        for strip in range(strips - FLIGHT, strips):
            relay_copy(strip, following).wait_send()

    @pl.when(has_prev)
    def _():
        def arrive(strip):
            relay_copy(strip, previous).wait_recv()
            for side, present, device in sides:
                @pl.when(present)
                def _():
                    rim_copy(side, strip, device).start()
            rows, padded = strip_rows(strip, 0), strip_rows(strip, PAD)
            for plane in range(count):
                relay_coeff[1 + plane, padded, :] = coefficient(
                    relay[1 + plane, padded, :], scaled[low + plane, rows, :]
                )

        def advance(strip):
            rows, padded = strip_rows(strip, 0), strip_rows(strip, PAD)
            for side, present, device in sides:
                @pl.when(present)
                def _():
                    rim_copy(1 - side, strip, device).wait_recv()
                at = (count + 1) * side
                relay_coeff[at, padded, :] = coefficient(
                    relay[at, padded, :], scaled[low - 1 + at, rows, :]
                )

            def emit(plane, value, increment):
                result = out[plane - 1, rows, :] + (value + coarse * increment)

                def store():
                    out[plane - 1, rows, :] = result

                return store

            sweep(relay, relay_coeff, range(1, count + 1), padded.start, STRIP, emit)

            @pl.when(has_next)
            def _():
                relay_copy(strip, following).start()

        for strip in range(LAG):
            arrive(strip)

        def turn(strip, _):
            arrive(strip)
            advance(strip - LAG)
            return 0

        lax.fori_loop(LAG, strips, turn, 0)
        for strip in range(strips - LAG, strips):
            advance(strip)

        def finish(strip, _):
            for side, present, device in sides:
                @pl.when(present)
                def _():
                    rim_copy(side, strip, device).wait_send()
            return 0

        lax.fori_loop(0, strips, finish, 0)

    @pl.when(jnp.logical_and(has_prev, has_next))
    def _():
        def finish(strip, _):
            relay_copy(strip, following).wait_send()
            return 0

        lax.fori_loop(0, strips, finish, 0)


def per_device(slices, blocks, start_values, regions, resistivity):
    start = start_values[0]
    count, height, lanes = start.shape
    tall, deep = height + 2 * PAD, count + 2 * WIDTH
    strips = height // STRIP
    dma, vmem = pltpu.SemaphoreType.DMA, pltpu.VMEM
    f32 = jnp.float32
    result = pl.pallas_call(
        functools.partial(kernel, slices, blocks),
        out_shape=jax.ShapeDtypeStruct(start.shape, f32),
        in_specs=[
            pl.BlockSpec(memory_space=pltpu.HBM),
            pl.BlockSpec(memory_space=pltpu.HBM),
            pl.BlockSpec(memory_space=pltpu.HBM),
        ],
        out_specs=pl.BlockSpec(memory_space=pltpu.VMEM),
        scratch_shapes=[
            vmem(start.shape, f32),
            vmem(regions.shape, regions.dtype),
            pltpu.SMEM(resistivity.shape, f32),
            *[vmem((deep, tall, lanes), f32) for _ in range(4)],
            vmem((deep, height, lanes), f32),
            vmem((2, 2, WIDTH, height, lanes), f32),
            vmem(start.shape, f32),
            vmem((count + 2, tall, lanes), f32),
            vmem((count + 2, tall, lanes), f32),
            dma((3,)), dma((2, 2)), dma((2, 2)), dma((2,)), dma((2,)),
            dma((strips,)), dma((strips,)), dma((2, strips)), dma((2, strips)),
        ],
        compiler_params=pltpu.CompilerParams(
            collective_id=0, has_side_effects=True, vmem_limit_bytes=64 * 2**20
        ),
        cost_estimate=pl.CostEstimate(flops=start.size * 400, bytes_accessed=start.size * 12, transcendentals=0),
    )(start, regions, resistivity)
    return result[None]


def solution(mesh):
    in_specs = (P("tm", "space", None, None), P("space", None, None), P())
    out_specs = P("tm", "space", None, None)
    return jax.shard_map(
        functools.partial(per_device, mesh.shape["tm"], mesh.shape["space"]),
        mesh=mesh, in_specs=in_specs, out_specs=out_specs, check_vma=False,
    )
```

```python
import functools

import jax
import jax.numpy as jnp
from jax import lax
from jax.experimental import pallas as pl
from jax.experimental.pallas import tpu as pltpu
from jax.sharding import PartitionSpec as P

STEPS = 8
fine_step = 0.008
WIDTH = 4
PAD = 8
CHUNK = 32
STRIP = 8
LAG = 1
FLIGHT = 3
HELD = 2
MESH = pl.DeviceIdType.MESH


def coefficient(field, scaled):
    denominator = 1.0 + field * field
    estimate = pl.reciprocal(denominator, approx=True)
    inverse = estimate * (2.0 - denominator * estimate)
    return scaled * (2.0 - inverse)


def sweep(field_at, coeff_at, planes, row, count, emit):
    rows = pl.ds(row, count)
    lane = lax.broadcasted_iota(jnp.int32, (count, field_at.shape[-1]), 1)
    lanes = field_at.shape[-1]
    is_first, is_last = lane == 0, lane == lanes - 1
    low = planes.start
    before, here = field_at[low - 1, rows, :], field_at[low, rows, :]
    k_before, k_here = coeff_at[low - 1, rows, :], coeff_at[low, rows, :]
    flux_before = (k_before + k_here) * (here - before)
    held = []
    for plane in planes:
        after, k_after = field_at[plane + 1, rows, :], coeff_at[plane + 1, rows, :]
        flux = (k_here + k_after) * (after - here)
        total = flux - flux_before
        for shift in (-1, 1):
            near = pl.ds(row + shift, count)
            total += (k_here + coeff_at[plane, near, :]) * (field_at[plane, near, :] - here)
        right = jnp.where(is_last, 0.0, pltpu.roll(here, lanes - 1, 1))
        k_right = jnp.where(is_last, 0.0, pltpu.roll(k_here, lanes - 1, 1))
        across = (k_here + k_right) * (right - here)
        total += across - jnp.where(is_first, k_here * here, pltpu.roll(across, 1, 1))
        held.append(emit(plane, here, total))
        if len(held) > HELD:
            held.pop(0)()
        here, k_here, flux_before = after, k_after, flux
    for store in held:
        store()


def kernel(
    slices, blocks, start_hbm, regions_hbm, resistivity_hbm, out,
    start, regions, resistivity, field_even, field_odd, coeff_even, coeff_odd,
    scaled, halo, outgoing, guess, relay, relay_coeff, input_sem,
    halo_send, halo_recv, scaled_send, scaled_recv, relay_send, relay_recv, rim_send, rim_recv,
):
    count, height, lanes = start.shape
    field, coeff = (field_even, field_odd), (coeff_even, coeff_odd)
    inputs = [
        pltpu.make_async_copy(source, target, input_sem.at[index])
        for index, (source, target) in enumerate(
            ((resistivity_hbm, resistivity), (regions_hbm, regions), (start_hbm, start))
        )
    ]
    for copy in inputs:
        copy.start()
    low, high = WIDTH, WIDTH + count
    me_t, me_s = lax.axis_index("tm"), lax.axis_index("space")
    has_low, has_high = me_s > 0, me_s < blocks - 1
    has_prev, has_next = me_t > 0, me_t < slices - 1
    below, above = (me_t, me_s - 1), (me_t, me_s + 1)
    previous, following = (me_t - 1, me_s), (me_t + 1, me_s)
    sides = ((0, has_low, below), (1, has_high, above))

    def chunks(body, size=CHUNK):
        def turn(index, _):
            body(pl.multiple_of(index * size, size))
            return 0

        lax.fori_loop(0, height // size, turn, 0)

    for buffer in (*field, *coeff, relay, relay_coeff):
        edge = jnp.zeros((buffer.shape[0], PAD, lanes), jnp.float32)
        buffer[:, pl.ds(0, PAD), :] = edge
        buffer[:, pl.ds(PAD + height, PAD), :] = edge
    for side, present, _ in sides:
        @pl.when(jnp.logical_not(present))
        def _():
            halo[:, side] = jnp.zeros((2, WIDTH, height, lanes), jnp.float32)
            scaled[pl.ds(high * side, WIDTH)] = jnp.zeros((WIDTH, height, lanes), jnp.float32)
            relay[(count + 1) * side, pl.ds(PAD, height), :] = jnp.zeros((height, lanes), jnp.float32)

    barrier = pltpu.get_barrier_semaphore()
    partners = [(has_low, below), (has_high, above), (has_prev, previous), (has_next, following)]
    for in_time, step in ((has_prev, -1), (has_next, 1)):
        for present, move in ((has_low, -1), (has_high, 1)):
            partners.append((jnp.logical_and(in_time, present), (me_t + step, me_s + move)))
    for present, target in partners:
        @pl.when(present)
        def _():
            pl.semaphore_signal(barrier, inc=1, device_id=target, device_id_type=MESH)
    pl.semaphore_wait(barrier, sum(jnp.where(present, 1, 0) for present, _ in partners))

    def remote(source, target, send_sem, recv_sem, device):
        return pltpu.make_async_remote_copy(
            src_ref=source, dst_ref=target, send_sem=send_sem, recv_sem=recv_sem,
            device_id=device, device_id_type=MESH,
        )

    def halo_copy(side, device, slot, source):
        return remote(
            source.at[pl.ds((count - WIDTH) * side, WIDTH)], halo.at[slot, 1 - side],
            halo_send.at[slot, side], halo_recv.at[slot, 1 - side], device,
        )

    def scaled_copy(side, device):
        return remote(
            scaled.at[pl.ds(low + (count - WIDTH) * side, WIDTH)],
            scaled.at[pl.ds(high * (1 - side), WIDTH)],
            scaled_send.at[side], scaled_recv.at[1 - side], device,
        )

    for side, present, device in sides:
        @pl.when(present)
        def _():
            halo_copy(side, device, 0, start_hbm).start()

    def lookup(plane, rows):
        region = regions[plane, rows, :]
        value = jnp.zeros(region.shape, jnp.float32)
        for index in range(resistivity.shape[0]):
            value = jnp.where(region == index, resistivity[index] * (0.5 * fine_step), value)
        return value

    order = list(range(WIDTH)) + list(range(count - WIDTH, count))

    def outer_scaled(row):
        for plane in order:
            scaled[low + plane, pl.ds(row, CHUNK), :] = lookup(plane, pl.ds(row, CHUNK))

    inputs[0].wait()
    inputs[1].wait()
    chunks(outer_scaled)
    for side, present, device in sides:
        @pl.when(present)
        def _():
            scaled_copy(side, device).start()

    def prepare(row):
        rows, padded = pl.ds(row, CHUNK), pl.ds(row + PAD, CHUNK)
        for plane in range(count):
            value = start[plane, rows, :]
            if plane in order:
                factor = scaled[low + plane, rows, :]
            else:
                factor = lookup(plane, rows)
                scaled[low + plane, rows, :] = factor
            field_even[low + plane, padded, :] = value
            coeff_even[low + plane, padded, :] = coefficient(value, factor)

    inputs[2].wait()
    chunks(prepare)

    coarse = jnp.float32(STEPS)
    subtract = jnp.where(has_prev, 1.0, 0.0).astype(jnp.float32)
    keep = (jnp.where(has_low, 1.0, 0.0).astype(jnp.float32), jnp.where(has_high, 1.0, 0.0).astype(jnp.float32))

    def fine(step, now, planes):
        if not planes:
            return
        later = 1 - now
        first, last = step == 0, step == STEPS - 1

        def body(row):
            def emit(plane, value, increment):
                rows, padded = pl.ds(row, CHUNK), pl.ds(row + PAD, CHUNK)
                own = low <= plane < high
                stepped = value + increment
                if last:
                    result = stepped - guess[plane - low, rows, :]

                    def store_last():
                        out[plane - low, rows, :] = result

                    return store_last
                if not own:
                    stepped = stepped * keep[0 if plane < low else 1]
                factor = coefficient(stepped, scaled[plane, rows, :])

                def store():
                    if first and own:
                        guess[plane - low, rows, :] = subtract * (value + coarse * increment)
                    if own and step % WIDTH == WIDTH - 1:
                        outgoing[plane - low, rows, :] = stepped
                    field[later][plane, padded, :] = stepped
                    coeff[later][plane, padded, :] = factor

                return store

            sweep(field[now], coeff[now], planes, row + PAD, CHUNK, emit)

        chunks(body)

    rounds = STEPS // WIDTH
    is_even = lax.rem(me_s, 2) == 0
    for turn in range(rounds):
        slot = turn % 2
        source = start_hbm if turn == 0 else outgoing
        for inside in range(WIDTH):
            fine(turn * WIDTH + inside, inside % 2, range(low + inside + 1, high - inside - 1))
        def finish_side(side, present, device, turn=turn, slot=slot, source=source):
            @pl.when(present)
            def _():
                copy = halo_copy(side, device, slot, source)
                copy.wait_send()
                if turn == 0:
                    scaled_copy(side, device).wait_send()
                    scaled_copy(1 - side, device).wait_recv()
                halo_copy(1 - side, device, slot, source).wait_recv()

            def place(row, side=side):
                rows, padded = pl.ds(row, CHUNK), pl.ds(row + PAD, CHUNK)
                for plane in range(WIDTH):
                    at = high * side + plane
                    value = halo[slot, side, plane, rows, :]
                    field_even[at, padded, :] = value
                    coeff_even[at, padded, :] = coefficient(value, scaled[at, rows, :])

            chunks(place)
            for inside in range(WIDTH):
                reach = WIDTH - 1 - inside
                if side == 0:
                    planes = range(low - reach, low + inside + 1)
                else:
                    planes = range(high - inside - 1, high + reach)
                fine(turn * WIDTH + inside, inside % 2, planes)
            if turn < rounds - 1:
                @pl.when(present)
                def _():
                    halo_copy(side, device, 1 - slot, outgoing).start()

        @pl.when(is_even)
        def _():
            for side in reversed(sides):
                finish_side(*side)

        @pl.when(jnp.logical_not(is_even))
        def _():
            for side in sides:
                finish_side(*side)

    strips = height // STRIP

    def strip_rows(strip, offset):
        return pl.ds(pl.multiple_of(strip * STRIP + offset, STRIP if offset % STRIP == 0 else 8), STRIP)

    def relay_copy(strip, device):
        return remote(
            out.at[:, strip_rows(strip, 0), :],
            relay.at[pl.ds(1, count), strip_rows(strip, PAD), :],
            relay_send.at[strip], relay_recv.at[strip], device,
        )

    def rim_copy(side, strip, device):
        rows = strip_rows(strip, PAD)
        return remote(
            out.at[(count - 1) * side, strip_rows(strip, 0), :],
            relay.at[(count + 1) * (1 - side), rows, :],
            rim_send.at[side, strip], rim_recv.at[1 - side, strip], device,
        )

    def send_strip(strip):
        for side, present, device in sides:
            @pl.when(present)
            def _():
                rim_copy(side, strip, (device[0] + 1, device[1])).start()
        relay_copy(strip, following).start()

    def finish_strip(strip):
        for side, present, device in sides:
            @pl.when(present)
            def _():
                rim_copy(side, strip, (device[0] + 1, device[1])).wait_send()
        relay_copy(strip, following).wait_send()

    @pl.when(jnp.logical_not(has_prev))
    def _():
        for strip in range(FLIGHT):
            send_strip(strip)

        def send(strip, _):
            finish_strip(strip - FLIGHT)
            send_strip(strip)
            return 0

        lax.fori_loop(FLIGHT, strips, send, 0)
        for strip in range(strips - FLIGHT, strips):
            finish_strip(strip)

    @pl.when(has_prev)
    def _():
        def arrive(strip):
            relay_copy(strip, previous).wait_recv()
            rows, padded = strip_rows(strip, 0), strip_rows(strip, PAD)
            for plane in range(count):
                relay_coeff[1 + plane, padded, :] = coefficient(
                    relay[1 + plane, padded, :], scaled[low + plane, rows, :]
                )

        def advance(strip):
            rows, padded = strip_rows(strip, 0), strip_rows(strip, PAD)
            for side, present, device in sides:
                @pl.when(present)
                def _():
                    rim_copy(1 - side, strip, device).wait_recv()
                at = (count + 1) * side
                relay_coeff[at, padded, :] = coefficient(
                    relay[at, padded, :], scaled[low - 1 + at, rows, :]
                )

            def emit(plane, value, increment):
                result = out[plane - 1, rows, :] + (value + coarse * increment)

                def store():
                    out[plane - 1, rows, :] = result

                return store

            sweep(relay, relay_coeff, range(1, count + 1), padded.start, STRIP, emit)

            @pl.when(has_next)
            def _():
                send_strip(strip)

        for strip in range(LAG):
            arrive(strip)

        def turn(strip, _):
            arrive(strip)
            advance(strip - LAG)
            return 0

        lax.fori_loop(LAG, strips, turn, 0)
        for strip in range(strips - LAG, strips):
            advance(strip)

    @pl.when(jnp.logical_and(has_prev, has_next))
    def _():
        def finish(strip, _):
            finish_strip(strip)
            return 0

        lax.fori_loop(0, strips, finish, 0)


def per_device(slices, blocks, start_values, regions, resistivity):
    start = start_values[0]
    count, height, lanes = start.shape
    tall, deep = height + 2 * PAD, count + 2 * WIDTH
    strips = height // STRIP
    dma, vmem = pltpu.SemaphoreType.DMA, pltpu.VMEM
    f32 = jnp.float32
    result = pl.pallas_call(
        functools.partial(kernel, slices, blocks),
        out_shape=jax.ShapeDtypeStruct(start.shape, f32),
        in_specs=[
            pl.BlockSpec(memory_space=pltpu.HBM),
            pl.BlockSpec(memory_space=pltpu.HBM),
            pl.BlockSpec(memory_space=pltpu.HBM),
        ],
        out_specs=pl.BlockSpec(memory_space=pltpu.VMEM),
        scratch_shapes=[
            vmem(start.shape, f32),
            vmem(regions.shape, regions.dtype),
            pltpu.SMEM(resistivity.shape, f32),
            *[vmem((deep, tall, lanes), f32) for _ in range(4)],
            vmem((deep, height, lanes), f32),
            vmem((2, 2, WIDTH, height, lanes), f32),
            vmem(start.shape, f32),
            vmem(start.shape, f32),
            vmem((count + 2, tall, lanes), f32),
            vmem((count + 2, tall, lanes), f32),
            dma((3,)), dma((2, 2)), dma((2, 2)), dma((2,)), dma((2,)),
            dma((strips,)), dma((strips,)), dma((2, strips)), dma((2, strips)),
        ],
        compiler_params=pltpu.CompilerParams(
            collective_id=0, has_side_effects=True, vmem_limit_bytes=64 * 2**20
        ),
        cost_estimate=pl.CostEstimate(flops=start.size * 400, bytes_accessed=start.size * 12, transcendentals=0),
    )(start, regions, resistivity)
    return result[None]


def solution(mesh):
    in_specs = (P("tm", "space", None, None), P("space", None, None), P())
    out_specs = P("tm", "space", None, None)
    return jax.shard_map(
        functools.partial(per_device, mesh.shape["tm"], mesh.shape["space"]),
        mesh=mesh, in_specs=in_specs, out_specs=out_specs, check_vma=False,
    )
```

```python
import functools

import jax
import jax.numpy as jnp
from jax import lax
from jax.experimental import pallas as pl
from jax.experimental.pallas import tpu as pltpu
from jax.sharding import PartitionSpec as P

STEPS = 8
fine_step = 0.008
WIDTH = 4
PAD = 8
CHUNK = 32
STRIP = 8
LAG = 1
FLIGHT = 3
HELD = 2
MESH = pl.DeviceIdType.MESH


def coefficient(field, scaled):
    denominator = 1.0 + field * field
    estimate = pl.reciprocal(denominator, approx=True)
    inverse = estimate * (2.0 - denominator * estimate)
    return scaled * (2.0 - inverse)


def sweep(field_at, coeff_at, planes, row, count, emit):
    rows = pl.ds(row, count)
    lane = lax.broadcasted_iota(jnp.int32, (count, field_at.shape[-1]), 1)
    lanes = field_at.shape[-1]
    is_first, is_last = lane == 0, lane == lanes - 1
    low = planes.start
    before, here = field_at[low - 1, rows, :], field_at[low, rows, :]
    k_before, k_here = coeff_at[low - 1, rows, :], coeff_at[low, rows, :]
    flux_before = (k_before + k_here) * (here - before)
    held = []
    for plane in planes:
        after, k_after = field_at[plane + 1, rows, :], coeff_at[plane + 1, rows, :]
        flux = (k_here + k_after) * (after - here)
        total = flux - flux_before
        for shift in (-1, 1):
            near = pl.ds(row + shift, count)
            total += (k_here + coeff_at[plane, near, :]) * (field_at[plane, near, :] - here)
        right = jnp.where(is_last, 0.0, pltpu.roll(here, lanes - 1, 1))
        k_right = jnp.where(is_last, 0.0, pltpu.roll(k_here, lanes - 1, 1))
        across = (k_here + k_right) * (right - here)
        total += across - jnp.where(is_first, k_here * here, pltpu.roll(across, 1, 1))
        held.append(emit(plane, here, total))
        if len(held) > HELD:
            held.pop(0)()
        here, k_here, flux_before = after, k_after, flux
    for store in held:
        store()


def kernel(
    slices, blocks, start_hbm, regions_hbm, resistivity_hbm, out,
    start, regions, resistivity, field_even, field_odd, coeff_even, coeff_odd,
    scaled, halo, outgoing, guess, relay, relay_coeff, input_sem,
    halo_send, halo_recv, scaled_send, scaled_recv, relay_send, relay_recv, rim_send, rim_recv,
):
    count, height, lanes = start.shape
    field, coeff = (field_even, field_odd), (coeff_even, coeff_odd)
    inputs = [
        pltpu.make_async_copy(source, target, input_sem.at[index])
        for index, (source, target) in enumerate(
            ((resistivity_hbm, resistivity), (regions_hbm, regions), (start_hbm, start))
        )
    ]
    for copy in inputs:
        copy.start()
    low, high = WIDTH, WIDTH + count
    me_t, me_s = lax.axis_index("tm"), lax.axis_index("space")
    has_low, has_high = me_s > 0, me_s < blocks - 1
    has_prev, has_next = me_t > 0, me_t < slices - 1
    below, above = (me_t, me_s - 1), (me_t, me_s + 1)
    previous, following = (me_t - 1, me_s), (me_t + 1, me_s)
    sides = ((0, has_low, below), (1, has_high, above))

    def chunks(body, size=CHUNK):
        for index in range(height // size):
            body(index * size)

    for buffer in (*field, *coeff, relay, relay_coeff):
        edge = jnp.zeros((buffer.shape[0], PAD, lanes), jnp.float32)
        buffer[:, pl.ds(0, PAD), :] = edge
        buffer[:, pl.ds(PAD + height, PAD), :] = edge
    for side, present, _ in sides:
        @pl.when(jnp.logical_not(present))
        def _():
            halo[:, side] = jnp.zeros((2, WIDTH, height, lanes), jnp.float32)
            scaled[pl.ds(high * side, WIDTH)] = jnp.zeros((WIDTH, height, lanes), jnp.float32)
            relay[(count + 1) * side, pl.ds(PAD, height), :] = jnp.zeros((height, lanes), jnp.float32)

    barrier = pltpu.get_barrier_semaphore()
    partners = [(has_low, below), (has_high, above), (has_prev, previous), (has_next, following)]
    for in_time, step in ((has_prev, -1), (has_next, 1)):
        for present, move in ((has_low, -1), (has_high, 1)):
            partners.append((jnp.logical_and(in_time, present), (me_t + step, me_s + move)))
    for present, target in partners:
        @pl.when(present)
        def _():
            pl.semaphore_signal(barrier, inc=1, device_id=target, device_id_type=MESH)
    pl.semaphore_wait(barrier, sum(jnp.where(present, 1, 0) for present, _ in partners))

    def remote(source, target, send_sem, recv_sem, device):
        return pltpu.make_async_remote_copy(
            src_ref=source, dst_ref=target, send_sem=send_sem, recv_sem=recv_sem,
            device_id=device, device_id_type=MESH,
        )

    def halo_copy(side, device, slot, source):
        return remote(
            source.at[pl.ds((count - WIDTH) * side, WIDTH)], halo.at[slot, 1 - side],
            halo_send.at[slot, side], halo_recv.at[slot, 1 - side], device,
        )

    def scaled_copy(side, device):
        return remote(
            scaled.at[pl.ds(low + (count - WIDTH) * side, WIDTH)],
            scaled.at[pl.ds(high * (1 - side), WIDTH)],
            scaled_send.at[side], scaled_recv.at[1 - side], device,
        )

    for side, present, device in sides:
        @pl.when(present)
        def _():
            halo_copy(side, device, 0, start_hbm).start()

    def lookup(plane, rows):
        region = regions[plane, rows, :]
        value = jnp.zeros(region.shape, jnp.float32)
        for index in range(resistivity.shape[0]):
            value = jnp.where(region == index, resistivity[index] * (0.5 * fine_step), value)
        return value

    order = list(range(WIDTH)) + list(range(count - WIDTH, count))

    def outer_scaled(row):
        for plane in order:
            scaled[low + plane, pl.ds(row, CHUNK), :] = lookup(plane, pl.ds(row, CHUNK))

    inputs[0].wait()
    inputs[1].wait()
    chunks(outer_scaled)
    for side, present, device in sides:
        @pl.when(present)
        def _():
            scaled_copy(side, device).start()

    def prepare(row):
        rows, padded = pl.ds(row, CHUNK), pl.ds(row + PAD, CHUNK)
        for plane in range(count):
            value = start[plane, rows, :]
            if plane in order:
                factor = scaled[low + plane, rows, :]
            else:
                factor = lookup(plane, rows)
                scaled[low + plane, rows, :] = factor
            field_even[low + plane, padded, :] = value
            coeff_even[low + plane, padded, :] = coefficient(value, factor)

    inputs[2].wait()
    chunks(prepare)

    coarse = jnp.float32(STEPS)
    subtract = jnp.where(has_prev, 1.0, 0.0).astype(jnp.float32)
    keep = (jnp.where(has_low, 1.0, 0.0).astype(jnp.float32), jnp.where(has_high, 1.0, 0.0).astype(jnp.float32))

    def fine(step, now, planes):
        if not planes:
            return
        later = 1 - now
        first, last = step == 0, step == STEPS - 1

        def body(row):
            def emit(plane, value, increment):
                rows, padded = pl.ds(row, CHUNK), pl.ds(row + PAD, CHUNK)
                own = low <= plane < high
                stepped = value + increment
                if last:
                    result = stepped - guess[plane - low, rows, :]

                    def store_last():
                        out[plane - low, rows, :] = result

                    return store_last
                if not own:
                    stepped = stepped * keep[0 if plane < low else 1]
                factor = coefficient(stepped, scaled[plane, rows, :])

                def store():
                    if first and own:
                        guess[plane - low, rows, :] = subtract * (value + coarse * increment)
                    if own and step % WIDTH == WIDTH - 1:
                        outgoing[plane - low, rows, :] = stepped
                    field[later][plane, padded, :] = stepped
                    coeff[later][plane, padded, :] = factor

                return store

            sweep(field[now], coeff[now], planes, row + PAD, CHUNK, emit)

        chunks(body)

    rounds = STEPS // WIDTH
    is_even = lax.rem(me_s, 2) == 0
    for turn in range(rounds):
        slot = turn % 2
        source = start_hbm if turn == 0 else outgoing
        for inside in range(WIDTH):
            fine(turn * WIDTH + inside, inside % 2, range(low + inside + 1, high - inside - 1))
        def finish_side(side, present, device, turn=turn, slot=slot, source=source):
            @pl.when(present)
            def _():
                copy = halo_copy(side, device, slot, source)
                copy.wait_send()
                if turn == 0:
                    scaled_copy(side, device).wait_send()
                    scaled_copy(1 - side, device).wait_recv()
                halo_copy(1 - side, device, slot, source).wait_recv()

            def place(row, side=side):
                rows, padded = pl.ds(row, CHUNK), pl.ds(row + PAD, CHUNK)
                for plane in range(WIDTH):
                    at = high * side + plane
                    value = halo[slot, side, plane, rows, :]
                    field_even[at, padded, :] = value
                    coeff_even[at, padded, :] = coefficient(value, scaled[at, rows, :])

            chunks(place)
            for inside in range(WIDTH):
                reach = WIDTH - 1 - inside
                if side == 0:
                    planes = range(low - reach, low + inside + 1)
                else:
                    planes = range(high - inside - 1, high + reach)
                fine(turn * WIDTH + inside, inside % 2, planes)
            if turn < rounds - 1:
                @pl.when(present)
                def _():
                    halo_copy(side, device, 1 - slot, outgoing).start()

        @pl.when(is_even)
        def _():
            for side in reversed(sides):
                finish_side(*side)

        @pl.when(jnp.logical_not(is_even))
        def _():
            for side in sides:
                finish_side(*side)

    strips = height // STRIP

    def strip_rows(strip, offset):
        return pl.ds(pl.multiple_of(strip * STRIP + offset, STRIP if offset % STRIP == 0 else 8), STRIP)

    def relay_copy(strip, device):
        return remote(
            out.at[:, strip_rows(strip, 0), :],
            relay.at[pl.ds(1, count), strip_rows(strip, PAD), :],
            relay_send.at[strip], relay_recv.at[strip], device,
        )

    def rim_copy(side, strip, device):
        rows = strip_rows(strip, PAD)
        return remote(
            out.at[(count - 1) * side, strip_rows(strip, 0), :],
            relay.at[(count + 1) * (1 - side), rows, :],
            rim_send.at[side, strip], rim_recv.at[1 - side, strip], device,
        )

    def send_strip(strip):
        for side, present, device in sides:
            @pl.when(present)
            def _():
                rim_copy(side, strip, (device[0] + 1, device[1])).start()
        relay_copy(strip, following).start()

    def finish_strip(strip):
        for side, present, device in sides:
            @pl.when(present)
            def _():
                rim_copy(side, strip, (device[0] + 1, device[1])).wait_send()
        relay_copy(strip, following).wait_send()

    @pl.when(jnp.logical_not(has_prev))
    def _():
        for strip in range(FLIGHT):
            send_strip(strip)

        def send(strip, _):
            finish_strip(strip - FLIGHT)
            send_strip(strip)
            return 0

        lax.fori_loop(FLIGHT, strips, send, 0)
        for strip in range(strips - FLIGHT, strips):
            finish_strip(strip)

    @pl.when(has_prev)
    def _():
        def arrive(strip):
            relay_copy(strip, previous).wait_recv()
            rows, padded = strip_rows(strip, 0), strip_rows(strip, PAD)
            for plane in range(count):
                relay_coeff[1 + plane, padded, :] = coefficient(
                    relay[1 + plane, padded, :], scaled[low + plane, rows, :]
                )

        def advance(strip):
            rows, padded = strip_rows(strip, 0), strip_rows(strip, PAD)
            for side, present, device in sides:
                @pl.when(present)
                def _():
                    rim_copy(1 - side, strip, device).wait_recv()
                at = (count + 1) * side
                relay_coeff[at, padded, :] = coefficient(
                    relay[at, padded, :], scaled[low - 1 + at, rows, :]
                )

            def emit(plane, value, increment):
                result = out[plane - 1, rows, :] + (value + coarse * increment)

                def store():
                    out[plane - 1, rows, :] = result

                return store

            sweep(relay, relay_coeff, range(1, count + 1), padded.start, STRIP, emit)

            @pl.when(has_next)
            def _():
                send_strip(strip)

        for strip in range(LAG):
            arrive(strip)

        def turn(strip, _):
            arrive(strip)
            advance(strip - LAG)
            return 0

        lax.fori_loop(LAG, strips, turn, 0)
        for strip in range(strips - LAG, strips):
            advance(strip)

    @pl.when(jnp.logical_and(has_prev, has_next))
    def _():
        def finish(strip, _):
            finish_strip(strip)
            return 0

        lax.fori_loop(0, strips, finish, 0)


def per_device(slices, blocks, start_values, regions, resistivity):
    start = start_values[0]
    count, height, lanes = start.shape
    tall, deep = height + 2 * PAD, count + 2 * WIDTH
    strips = height // STRIP
    dma, vmem = pltpu.SemaphoreType.DMA, pltpu.VMEM
    f32 = jnp.float32
    result = pl.pallas_call(
        functools.partial(kernel, slices, blocks),
        out_shape=jax.ShapeDtypeStruct(start.shape, f32),
        in_specs=[
            pl.BlockSpec(memory_space=pltpu.HBM),
            pl.BlockSpec(memory_space=pltpu.HBM),
            pl.BlockSpec(memory_space=pltpu.HBM),
        ],
        out_specs=pl.BlockSpec(memory_space=pltpu.VMEM),
        scratch_shapes=[
            vmem(start.shape, f32),
            vmem(regions.shape, regions.dtype),
            pltpu.SMEM(resistivity.shape, f32),
            *[vmem((deep, tall, lanes), f32) for _ in range(4)],
            vmem((deep, height, lanes), f32),
            vmem((2, 2, WIDTH, height, lanes), f32),
            vmem(start.shape, f32),
            vmem(start.shape, f32),
            vmem((count + 2, tall, lanes), f32),
            vmem((count + 2, tall, lanes), f32),
            dma((3,)), dma((2, 2)), dma((2, 2)), dma((2,)), dma((2,)),
            dma((strips,)), dma((strips,)), dma((2, strips)), dma((2, strips)),
        ],
        compiler_params=pltpu.CompilerParams(
            collective_id=0, has_side_effects=True, vmem_limit_bytes=64 * 2**20
        ),
        cost_estimate=pl.CostEstimate(flops=start.size * 400, bytes_accessed=start.size * 12, transcendentals=0),
    )(start, regions, resistivity)
    return result[None]


def solution(mesh):
    in_specs = (P("tm", "space", None, None), P("space", None, None), P())
    out_specs = P("tm", "space", None, None)
    return jax.shard_map(
        functools.partial(per_device, mesh.shape["tm"], mesh.shape["space"]),
        mesh=mesh, in_specs=in_specs, out_specs=out_specs, check_vma=False,
    )
```

```python
import functools

import jax
import jax.numpy as jnp
from jax import lax
from jax.experimental import pallas as pl
from jax.experimental.pallas import tpu as pltpu
from jax.sharding import PartitionSpec as P

STEPS = 8
fine_step = 0.008
WIDTH = 4
PAD = 8
CHUNK = 32
STRIP = 8
LAG = 1
FLIGHT = 3
HELD = 2
MESH = pl.DeviceIdType.MESH


def coefficient(field, scaled):
    denominator = 1.0 + field * field
    estimate = pl.reciprocal(denominator, approx=True)
    inverse = estimate * (2.0 - denominator * estimate)
    return scaled * (2.0 - inverse)


def sweep(field_at, coeff_at, low, number, row, count, emit):
    rows = pl.ds(row, count)
    lane = lax.broadcasted_iota(jnp.int32, (count, field_at.shape[-1]), 1)
    lanes = field_at.shape[-1]
    is_first, is_last = lane == 0, lane == lanes - 1
    before, here = field_at[low - 1, rows, :], field_at[low, rows, :]
    k_before, k_here = coeff_at[low - 1, rows, :], coeff_at[low, rows, :]
    flux_before = (k_before + k_here) * (here - before)
    held = []
    for position in range(number):
        plane = low + position
        after, k_after = field_at[plane + 1, rows, :], coeff_at[plane + 1, rows, :]
        flux = (k_here + k_after) * (after - here)
        total = flux - flux_before
        for shift in (-1, 1):
            near = pl.ds(row + shift, count)
            total += (k_here + coeff_at[plane, near, :]) * (field_at[plane, near, :] - here)
        right = jnp.where(is_last, 0.0, pltpu.roll(here, lanes - 1, 1))
        k_right = jnp.where(is_last, 0.0, pltpu.roll(k_here, lanes - 1, 1))
        across = (k_here + k_right) * (right - here)
        total += across - jnp.where(is_first, k_here * here, pltpu.roll(across, 1, 1))
        held.append(emit(position, here, total))
        if len(held) > HELD:
            held.pop(0)()
        here, k_here, flux_before = after, k_after, flux
    for store in held:
        store()


def kernel(
    slices, blocks, start_hbm, regions_hbm, resistivity_hbm, out,
    start, regions, resistivity, field_even, field_odd, coeff_even, coeff_odd,
    scaled, halo, outgoing, guess, relay, relay_coeff, input_sem,
    halo_send, halo_recv, scaled_send, scaled_recv, relay_send, relay_recv, rim_send, rim_recv,
):
    count, height, lanes = start.shape
    field, coeff = (field_even, field_odd), (coeff_even, coeff_odd)
    inputs = [
        pltpu.make_async_copy(source, target, input_sem.at[index])
        for index, (source, target) in enumerate(
            ((resistivity_hbm, resistivity), (regions_hbm, regions), (start_hbm, start))
        )
    ]
    for copy in inputs:
        copy.start()
    low, high = WIDTH, WIDTH + count
    me_t, me_s = lax.axis_index("tm"), lax.axis_index("space")
    has_low, has_high = me_s > 0, me_s < blocks - 1
    has_prev, has_next = me_t > 0, me_t < slices - 1
    below, above = (me_t, me_s - 1), (me_t, me_s + 1)
    previous, following = (me_t - 1, me_s), (me_t + 1, me_s)
    sides = ((0, has_low, below), (1, has_high, above))

    def chunks(body, size=CHUNK):
        def turn(index, _):
            body(pl.multiple_of(index * size, size))
            return 0

        lax.fori_loop(0, height // size, turn, 0)

    for buffer in (*field, *coeff, relay, relay_coeff):
        edge = jnp.zeros((buffer.shape[0], PAD, lanes), jnp.float32)
        buffer[:, pl.ds(0, PAD), :] = edge
        buffer[:, pl.ds(PAD + height, PAD), :] = edge
    for side, present, _ in sides:
        @pl.when(jnp.logical_not(present))
        def _():
            halo[:, side] = jnp.zeros((2, WIDTH, height, lanes), jnp.float32)
            scaled[pl.ds(high * side, WIDTH)] = jnp.zeros((WIDTH, height, lanes), jnp.float32)
            relay[(count + 1) * side, pl.ds(PAD, height), :] = jnp.zeros((height, lanes), jnp.float32)

    barrier = pltpu.get_barrier_semaphore()
    partners = [(has_low, below), (has_high, above), (has_prev, previous), (has_next, following)]
    for in_time, step in ((has_prev, -1), (has_next, 1)):
        for present, move in ((has_low, -1), (has_high, 1)):
            partners.append((jnp.logical_and(in_time, present), (me_t + step, me_s + move)))
    for present, target in partners:
        @pl.when(present)
        def _():
            pl.semaphore_signal(barrier, inc=1, device_id=target, device_id_type=MESH)
    pl.semaphore_wait(barrier, sum(jnp.where(present, 1, 0) for present, _ in partners))

    def remote(source, target, send_sem, recv_sem, device):
        return pltpu.make_async_remote_copy(
            src_ref=source, dst_ref=target, send_sem=send_sem, recv_sem=recv_sem,
            device_id=device, device_id_type=MESH,
        )

    def halo_copy(side, device, slot, source):
        return remote(
            source.at[pl.ds((count - WIDTH) * side, WIDTH)], halo.at[slot, 1 - side],
            halo_send.at[slot, side], halo_recv.at[slot, 1 - side], device,
        )

    def scaled_copy(side, device):
        return remote(
            scaled.at[pl.ds(low + (count - WIDTH) * side, WIDTH)],
            scaled.at[pl.ds(high * (1 - side), WIDTH)],
            scaled_send.at[side], scaled_recv.at[1 - side], device,
        )

    for side, present, device in sides:
        @pl.when(present)
        def _():
            halo_copy(side, device, 0, start_hbm).start()

    def lookup(plane, rows):
        region = regions[plane, rows, :]
        value = jnp.zeros(region.shape, jnp.float32)
        for index in range(resistivity.shape[0]):
            value = jnp.where(region == index, resistivity[index] * (0.5 * fine_step), value)
        return value

    order = list(range(WIDTH)) + list(range(count - WIDTH, count))

    def outer_scaled(row):
        for plane in order:
            scaled[low + plane, pl.ds(row, CHUNK), :] = lookup(plane, pl.ds(row, CHUNK))

    inputs[0].wait()
    inputs[1].wait()
    chunks(outer_scaled)
    for side, present, device in sides:
        @pl.when(present)
        def _():
            scaled_copy(side, device).start()

    def prepare(row):
        rows, padded = pl.ds(row, CHUNK), pl.ds(row + PAD, CHUNK)
        for plane in range(count):
            value = start[plane, rows, :]
            if plane in order:
                factor = scaled[low + plane, rows, :]
            else:
                factor = lookup(plane, rows)
                scaled[low + plane, rows, :] = factor
            field_even[low + plane, padded, :] = value
            coeff_even[low + plane, padded, :] = coefficient(value, factor)

    inputs[2].wait()
    chunks(prepare)

    coarse = jnp.float32(STEPS)
    subtract = jnp.where(has_prev, 1.0, 0.0).astype(jnp.float32)

    def fine(turn, inside, first, number, reach=0, side=None, present=None):
        if number <= 0:
            return
        now, later = inside % 2, 1 - inside % 2
        last = inside == WIDTH - 1

        def body(row):
            rows, padded = pl.ds(row, CHUNK), pl.ds(row + PAD, CHUNK)

            def emit(position, value, increment):
                plane = first + position
                stepped = value + increment
                if reach:
                    beyond = jnp.where(side == 0, position < reach, position > inside)
                    grid = jnp.logical_or(present, jnp.logical_not(beyond))
                    stepped = stepped * jnp.where(grid, 1.0, 0.0).astype(jnp.float32)
                factor = coefficient(stepped, scaled[plane, rows, :])
                if inside == 0:
                    ahead = subtract * (value + coarse * increment)
                    ahead = jnp.where(turn == 0, ahead, guess[plane, rows, :])
                if last:
                    result = stepped - guess[plane, rows, :]

                def store():
                    if inside == 0:
                        guess[plane, rows, :] = ahead
                    if last:
                        out[plane - low, rows, :] = result
                        outgoing[plane - low, rows, :] = stepped
                    field[later][plane, padded, :] = stepped
                    coeff[later][plane, padded, :] = factor

                return store

            sweep(field[now], coeff[now], first, number, row + PAD, CHUNK, emit)

        chunks(body)

    rounds = STEPS // WIDTH
    is_even = lax.rem(me_s, 2) == 0

    def one_round(turn, _):
        slot = lax.rem(turn, 2)
        for inside in range(WIDTH):
            fine(turn, inside, low + inside + 1, count - 2 * inside - 2)

        def finish_side(index, _):
            side = jnp.where(is_even, 1 - index, index)
            present = jnp.where(side == 0, has_low, has_high)
            device = (me_t, me_s + 2 * side - 1)

            @pl.when(present)
            def _():
                halo_copy(side, device, slot, outgoing).wait_send()
                halo_copy(1 - side, device, slot, outgoing).wait_recv()

            @pl.when(jnp.logical_and(present, turn == 0))
            def _():
                scaled_copy(side, device).wait_send()
                scaled_copy(1 - side, device).wait_recv()

            def place(row):
                rows, padded = pl.ds(row, CHUNK), pl.ds(row + PAD, CHUNK)
                for plane in range(WIDTH):
                    at = high * side + plane
                    value = halo[slot, side, plane, rows, :]
                    field_even[at, padded, :] = value
                    coeff_even[at, padded, :] = coefficient(value, scaled[at, rows, :])

            chunks(place)
            for inside in range(WIDTH):
                reach = WIDTH - 1 - inside
                first = jnp.where(side == 0, low - reach, high - inside - 1)
                fine(turn, inside, first, WIDTH, reach, side, present)

            @pl.when(jnp.logical_and(present, turn < rounds - 1))
            def _():
                halo_copy(side, device, 1 - slot, outgoing).start()

            return 0

        lax.fori_loop(0, 2, finish_side, 0)
        return 0

    lax.fori_loop(0, rounds, one_round, 0)

    strips = height // STRIP

    def strip_rows(strip, offset):
        return pl.ds(pl.multiple_of(strip * STRIP + offset, STRIP if offset % STRIP == 0 else 8), STRIP)

    def relay_copy(strip, device):
        return remote(
            out.at[:, strip_rows(strip, 0), :],
            relay.at[pl.ds(1, count), strip_rows(strip, PAD), :],
            relay_send.at[strip], relay_recv.at[strip], device,
        )

    def rim_copy(side, strip, device):
        rows = strip_rows(strip, PAD)
        return remote(
            out.at[(count - 1) * side, strip_rows(strip, 0), :],
            relay.at[(count + 1) * (1 - side), rows, :],
            rim_send.at[side, strip], rim_recv.at[1 - side, strip], device,
        )

    def send_strip(strip):
        for side, present, device in sides:
            @pl.when(present)
            def _():
                rim_copy(side, strip, (device[0] + 1, device[1])).start()
        relay_copy(strip, following).start()

    def finish_strip(strip):
        for side, present, device in sides:
            @pl.when(present)
            def _():
                rim_copy(side, strip, (device[0] + 1, device[1])).wait_send()
        relay_copy(strip, following).wait_send()

    @pl.when(jnp.logical_not(has_prev))
    def _():
        for strip in range(FLIGHT):
            send_strip(strip)

        def send(strip, _):
            finish_strip(strip - FLIGHT)
            send_strip(strip)
            return 0

        lax.fori_loop(FLIGHT, strips, send, 0)
        for strip in range(strips - FLIGHT, strips):
            finish_strip(strip)

    @pl.when(has_prev)
    def _():
        def arrive(strip):
            relay_copy(strip, previous).wait_recv()
            rows, padded = strip_rows(strip, 0), strip_rows(strip, PAD)
            for plane in range(count):
                relay_coeff[1 + plane, padded, :] = coefficient(
                    relay[1 + plane, padded, :], scaled[low + plane, rows, :]
                )

        def advance(strip):
            rows, padded = strip_rows(strip, 0), strip_rows(strip, PAD)
            for side, present, device in sides:
                @pl.when(present)
                def _():
                    rim_copy(1 - side, strip, device).wait_recv()
                at = (count + 1) * side
                relay_coeff[at, padded, :] = coefficient(
                    relay[at, padded, :], scaled[low - 1 + at, rows, :]
                )

            def emit(plane, value, increment):
                result = out[plane, rows, :] + (value + coarse * increment)

                def store():
                    out[plane, rows, :] = result

                return store

            sweep(relay, relay_coeff, 1, count, padded.start, STRIP, emit)

            @pl.when(has_next)
            def _():
                send_strip(strip)

        for strip in range(LAG):
            arrive(strip)

        def turn(strip, _):
            arrive(strip)
            advance(strip - LAG)
            return 0

        lax.fori_loop(LAG, strips, turn, 0)
        for strip in range(strips - LAG, strips):
            advance(strip)

    @pl.when(jnp.logical_and(has_prev, has_next))
    def _():
        def finish(strip, _):
            finish_strip(strip)
            return 0

        lax.fori_loop(0, strips, finish, 0)


def per_device(slices, blocks, start_values, regions, resistivity):
    start = start_values[0]
    count, height, lanes = start.shape
    tall, deep = height + 2 * PAD, count + 2 * WIDTH
    strips = height // STRIP
    dma, vmem = pltpu.SemaphoreType.DMA, pltpu.VMEM
    f32 = jnp.float32
    result = pl.pallas_call(
        functools.partial(kernel, slices, blocks),
        out_shape=jax.ShapeDtypeStruct(start.shape, f32),
        in_specs=[
            pl.BlockSpec(memory_space=pltpu.HBM),
            pl.BlockSpec(memory_space=pltpu.HBM),
            pl.BlockSpec(memory_space=pltpu.HBM),
        ],
        out_specs=pl.BlockSpec(memory_space=pltpu.VMEM),
        scratch_shapes=[
            vmem(start.shape, f32),
            vmem(regions.shape, regions.dtype),
            pltpu.SMEM(resistivity.shape, f32),
            *[vmem((deep, tall, lanes), f32) for _ in range(4)],
            vmem((deep, height, lanes), f32),
            vmem((2, 2, WIDTH, height, lanes), f32),
            vmem(start.shape, f32),
            vmem((deep, height, lanes), f32),
            vmem((count + 2, tall, lanes), f32),
            vmem((count + 2, tall, lanes), f32),
            dma((3,)), dma((2, 2)), dma((2, 2)), dma((2,)), dma((2,)),
            dma((strips,)), dma((strips,)), dma((2, strips)), dma((2, strips)),
        ],
        compiler_params=pltpu.CompilerParams(
            collective_id=0, has_side_effects=True, vmem_limit_bytes=64 * 2**20
        ),
        cost_estimate=pl.CostEstimate(flops=start.size * 400, bytes_accessed=start.size * 12, transcendentals=0),
    )(start, regions, resistivity)
    return result[None]


def solution(mesh):
    in_specs = (P("tm", "space", None, None), P("space", None, None), P())
    out_specs = P("tm", "space", None, None)
    return jax.shard_map(
        functools.partial(per_device, mesh.shape["tm"], mesh.shape["space"]),
        mesh=mesh, in_specs=in_specs, out_specs=out_specs, check_vma=False,
    )
```

```python
import functools

import jax
import jax.numpy as jnp
from jax import lax
from jax.experimental import pallas as pl
from jax.experimental.pallas import tpu as pltpu
from jax.sharding import PartitionSpec as P

STEPS = 8
fine_step = 0.008
WIDTH = 4
PAD = 8
CHUNK = 64
STRIP = 8
LAG = 1
FLIGHT = 3
HELD = 1
MESH = pl.DeviceIdType.MESH


def coefficient(field, scaled):
    denominator = 1.0 + field * field
    estimate = pl.reciprocal(denominator, approx=True)
    inverse = estimate * (2.0 - denominator * estimate)
    return scaled * (2.0 - inverse)


def sweep(field_at, coeff_at, low, number, row, count, emit):
    rows = pl.ds(row, count)
    lane = lax.broadcasted_iota(jnp.int32, (count, field_at.shape[-1]), 1)
    lanes = field_at.shape[-1]
    is_first, is_last = lane == 0, lane == lanes - 1
    before, here = field_at[low - 1, rows, :], field_at[low, rows, :]
    k_before, k_here = coeff_at[low - 1, rows, :], coeff_at[low, rows, :]
    flux_before = (k_before + k_here) * (here - before)
    held = []
    for position in range(number):
        plane = low + position
        after, k_after = field_at[plane + 1, rows, :], coeff_at[plane + 1, rows, :]
        flux = (k_here + k_after) * (after - here)
        total = flux - flux_before
        for shift in (-1, 1):
            near = pl.ds(row + shift, count)
            total += (k_here + coeff_at[plane, near, :]) * (field_at[plane, near, :] - here)
        right = jnp.where(is_last, 0.0, pltpu.roll(here, lanes - 1, 1))
        k_right = jnp.where(is_last, 0.0, pltpu.roll(k_here, lanes - 1, 1))
        across = (k_here + k_right) * (right - here)
        total += across - jnp.where(is_first, k_here * here, pltpu.roll(across, 1, 1))
        held.append(emit(position, here, total))
        if len(held) > HELD:
            held.pop(0)()
        here, k_here, flux_before = after, k_after, flux
    for store in held:
        store()


def kernel(
    slices, blocks, start_hbm, regions_hbm, resistivity_hbm, out,
    start, regions, resistivity, field_even, field_odd, coeff_even, coeff_odd,
    scaled, halo, outgoing, guess, relay, relay_coeff, input_sem,
    halo_send, halo_recv, scaled_send, scaled_recv, relay_send, relay_recv, rim_send, rim_recv,
):
    count, height, lanes = start.shape
    field, coeff = (field_even, field_odd), (coeff_even, coeff_odd)
    inputs = [
        pltpu.make_async_copy(source, target, input_sem.at[index])
        for index, (source, target) in enumerate(
            ((resistivity_hbm, resistivity), (regions_hbm, regions), (start_hbm, start))
        )
    ]
    for copy in inputs:
        copy.start()
    low, high = WIDTH, WIDTH + count
    me_t, me_s = lax.axis_index("tm"), lax.axis_index("space")
    has_low, has_high = me_s > 0, me_s < blocks - 1
    has_prev, has_next = me_t > 0, me_t < slices - 1
    below, above = (me_t, me_s - 1), (me_t, me_s + 1)
    previous, following = (me_t - 1, me_s), (me_t + 1, me_s)
    sides = ((0, has_low, below), (1, has_high, above))

    def chunks(body, size=CHUNK):
        def turn(index, _):
            body(pl.multiple_of(index * size, size))
            return 0

        lax.fori_loop(0, height // size, turn, 0)

    barrier = pltpu.get_barrier_semaphore()
    partners = [(has_low, below), (has_high, above), (has_prev, previous), (has_next, following)]
    for in_time, step in ((has_prev, -1), (has_next, 1)):
        for present, move in ((has_low, -1), (has_high, 1)):
            partners.append((jnp.logical_and(in_time, present), (me_t + step, me_s + move)))
    for present, target in partners:
        @pl.when(present)
        def _():
            pl.semaphore_signal(barrier, inc=1, device_id=target, device_id_type=MESH)
    for buffer in (*field, *coeff, relay, relay_coeff):
        edge = jnp.zeros((buffer.shape[0], PAD, lanes), jnp.float32)
        buffer[:, pl.ds(0, PAD), :] = edge
        buffer[:, pl.ds(PAD + height, PAD), :] = edge
    for side, present, _ in sides:
        @pl.when(jnp.logical_not(present))
        def _():
            halo[:, side] = jnp.zeros((2, WIDTH, height, lanes), jnp.float32)
            scaled[pl.ds(high * side, WIDTH)] = jnp.zeros((WIDTH, height, lanes), jnp.float32)
            relay[(count + 1) * side, pl.ds(PAD, height), :] = jnp.zeros((height, lanes), jnp.float32)

    pl.semaphore_wait(barrier, sum(jnp.where(present, 1, 0) for present, _ in partners))

    def remote(source, target, send_sem, recv_sem, device):
        return pltpu.make_async_remote_copy(
            src_ref=source, dst_ref=target, send_sem=send_sem, recv_sem=recv_sem,
            device_id=device, device_id_type=MESH,
        )

    def halo_copy(side, device, slot, source):
        return remote(
            source.at[pl.ds((count - WIDTH) * side, WIDTH)], halo.at[slot, 1 - side],
            halo_send.at[slot, side], halo_recv.at[slot, 1 - side], device,
        )

    def scaled_copy(side, device):
        return remote(
            scaled.at[pl.ds(low + (count - WIDTH) * side, WIDTH)],
            scaled.at[pl.ds(high * (1 - side), WIDTH)],
            scaled_send.at[side], scaled_recv.at[1 - side], device,
        )

    for side, present, device in sides:
        @pl.when(present)
        def _():
            halo_copy(side, device, 0, start_hbm).start()

    def lookup(plane, rows):
        region = regions[plane, rows, :]
        value = jnp.zeros(region.shape, jnp.float32)
        for index in range(resistivity.shape[0]):
            value = jnp.where(region == index, resistivity[index] * (0.5 * fine_step), value)
        return value

    order = list(range(WIDTH)) + list(range(count - WIDTH, count))

    def outer_scaled(row):
        for plane in order:
            scaled[low + plane, pl.ds(row, CHUNK), :] = lookup(plane, pl.ds(row, CHUNK))

    inputs[0].wait()
    inputs[1].wait()
    chunks(outer_scaled)
    for side, present, device in sides:
        @pl.when(present)
        def _():
            scaled_copy(side, device).start()

    def prepare(row):
        rows, padded = pl.ds(row, CHUNK), pl.ds(row + PAD, CHUNK)
        for plane in range(count):
            value = start[plane, rows, :]
            if plane in order:
                factor = scaled[low + plane, rows, :]
            else:
                factor = lookup(plane, rows)
                scaled[low + plane, rows, :] = factor
            field_even[low + plane, padded, :] = value
            coeff_even[low + plane, padded, :] = coefficient(value, factor)

    inputs[2].wait()
    chunks(prepare)

    coarse = jnp.float32(STEPS)
    subtract = jnp.where(has_prev, 1.0, 0.0).astype(jnp.float32)

    def fine(turn, inside, first, number, reach=0, side=None, present=None):
        if number <= 0:
            return
        now, later = inside % 2, 1 - inside % 2
        last = inside == WIDTH - 1

        def body(row):
            rows, padded = pl.ds(row, CHUNK), pl.ds(row + PAD, CHUNK)

            def emit(position, value, increment):
                plane = first + position
                stepped = value + increment
                if reach:
                    beyond = jnp.where(side == 0, position < reach, position > inside)
                    grid = jnp.logical_or(present, jnp.logical_not(beyond))
                    stepped = stepped * jnp.where(grid, 1.0, 0.0).astype(jnp.float32)
                factor = coefficient(stepped, scaled[plane, rows, :])
                if inside == 0:
                    ahead = subtract * (value + coarse * increment)
                    ahead = jnp.where(turn == 0, ahead, guess[plane, rows, :])
                if last:
                    result = stepped - guess[plane, rows, :]

                def store():
                    if inside == 0:
                        guess[plane, rows, :] = ahead
                    if last:
                        out[plane - low, rows, :] = result
                        outgoing[plane - low, rows, :] = stepped
                    field[later][plane, padded, :] = stepped
                    coeff[later][plane, padded, :] = factor

                return store

            sweep(field[now], coeff[now], first, number, row + PAD, CHUNK, emit)

        chunks(body)

    rounds = STEPS // WIDTH
    is_even = lax.rem(me_s, 2) == 0

    def one_round(turn, _):
        slot = lax.rem(turn, 2)
        for inside in range(WIDTH):
            fine(turn, inside, low + inside + 1, count - 2 * inside - 2)

        def finish_side(index, _):
            side = jnp.where(is_even, 1 - index, index)
            present = jnp.where(side == 0, has_low, has_high)
            device = (me_t, me_s + 2 * side - 1)

            @pl.when(present)
            def _():
                halo_copy(side, device, slot, outgoing).wait_send()
                halo_copy(1 - side, device, slot, outgoing).wait_recv()

            @pl.when(jnp.logical_and(present, turn == 0))
            def _():
                scaled_copy(side, device).wait_send()
                scaled_copy(1 - side, device).wait_recv()

            def place(row):
                rows, padded = pl.ds(row, CHUNK), pl.ds(row + PAD, CHUNK)
                for plane in range(WIDTH):
                    at = high * side + plane
                    value = halo[slot, side, plane, rows, :]
                    field_even[at, padded, :] = value
                    coeff_even[at, padded, :] = coefficient(value, scaled[at, rows, :])

            chunks(place)
            for inside in range(WIDTH):
                reach = WIDTH - 1 - inside
                first = jnp.where(side == 0, low - reach, high - inside - 1)
                fine(turn, inside, first, WIDTH, reach, side, present)

            @pl.when(jnp.logical_and(present, turn < rounds - 1))
            def _():
                halo_copy(side, device, 1 - slot, outgoing).start()

            return 0

        lax.fori_loop(0, 2, finish_side, 0)
        return 0

    lax.fori_loop(0, rounds, one_round, 0)

    strips = height // STRIP

    def strip_rows(strip, offset):
        return pl.ds(pl.multiple_of(strip * STRIP + offset, STRIP if offset % STRIP == 0 else 8), STRIP)

    def relay_copy(strip, device):
        return remote(
            out.at[:, strip_rows(strip, 0), :],
            relay.at[pl.ds(1, count), strip_rows(strip, PAD), :],
            relay_send.at[strip], relay_recv.at[strip], device,
        )

    def rim_copy(side, strip, device):
        rows = strip_rows(strip, PAD)
        return remote(
            out.at[(count - 1) * side, strip_rows(strip, 0), :],
            relay.at[(count + 1) * (1 - side), rows, :],
            rim_send.at[side, strip], rim_recv.at[1 - side, strip], device,
        )

    def send_strip(strip):
        for side, present, device in sides:
            @pl.when(present)
            def _():
                rim_copy(side, strip, (device[0] + 1, device[1])).start()
        relay_copy(strip, following).start()

    def finish_strip(strip):
        for side, present, device in sides:
            @pl.when(present)
            def _():
                rim_copy(side, strip, (device[0] + 1, device[1])).wait_send()
        relay_copy(strip, following).wait_send()

    @pl.when(jnp.logical_not(has_prev))
    def _():
        for strip in range(FLIGHT):
            send_strip(strip)

        def send(strip, _):
            finish_strip(strip - FLIGHT)
            send_strip(strip)
            return 0

        lax.fori_loop(FLIGHT, strips, send, 0)
        for strip in range(strips - FLIGHT, strips):
            finish_strip(strip)

    @pl.when(has_prev)
    def _():
        def arrive(strip):
            relay_copy(strip, previous).wait_recv()
            rows, padded = strip_rows(strip, 0), strip_rows(strip, PAD)
            for plane in range(count):
                relay_coeff[1 + plane, padded, :] = coefficient(
                    relay[1 + plane, padded, :], scaled[low + plane, rows, :]
                )

        def advance(strip):
            rows, padded = strip_rows(strip, 0), strip_rows(strip, PAD)
            for side, present, device in sides:
                @pl.when(present)
                def _():
                    rim_copy(1 - side, strip, device).wait_recv()
                at = (count + 1) * side
                relay_coeff[at, padded, :] = coefficient(
                    relay[at, padded, :], scaled[low - 1 + at, rows, :]
                )

            def emit(plane, value, increment):
                result = out[plane, rows, :] + (value + coarse * increment)

                def store():
                    out[plane, rows, :] = result

                return store

            sweep(relay, relay_coeff, 1, count, padded.start, STRIP, emit)

            @pl.when(has_next)
            def _():
                send_strip(strip)

        for strip in range(LAG):
            arrive(strip)

        def turn(strip, _):
            arrive(strip)
            advance(strip - LAG)
            return 0

        lax.fori_loop(LAG, strips, turn, 0)
        for strip in range(strips - LAG, strips):
            advance(strip)

    @pl.when(jnp.logical_and(has_prev, has_next))
    def _():
        def finish(strip, _):
            finish_strip(strip)
            return 0

        lax.fori_loop(0, strips, finish, 0)


def per_device(slices, blocks, start_values, regions, resistivity):
    start = start_values[0]
    count, height, lanes = start.shape
    tall, deep = height + 2 * PAD, count + 2 * WIDTH
    strips = height // STRIP
    dma, vmem = pltpu.SemaphoreType.DMA, pltpu.VMEM
    f32 = jnp.float32
    result = pl.pallas_call(
        functools.partial(kernel, slices, blocks),
        out_shape=jax.ShapeDtypeStruct(start.shape, f32),
        in_specs=[
            pl.BlockSpec(memory_space=pltpu.HBM),
            pl.BlockSpec(memory_space=pltpu.HBM),
            pl.BlockSpec(memory_space=pltpu.HBM),
        ],
        out_specs=pl.BlockSpec(memory_space=pltpu.VMEM),
        scratch_shapes=[
            vmem(start.shape, f32),
            vmem(regions.shape, regions.dtype),
            pltpu.SMEM(resistivity.shape, f32),
            *[vmem((deep, tall, lanes), f32) for _ in range(4)],
            vmem((deep, height, lanes), f32),
            vmem((2, 2, WIDTH, height, lanes), f32),
            vmem(start.shape, f32),
            vmem((deep, height, lanes), f32),
            vmem((count + 2, tall, lanes), f32),
            vmem((count + 2, tall, lanes), f32),
            dma((3,)), dma((2, 2)), dma((2, 2)), dma((2,)), dma((2,)),
            dma((strips,)), dma((strips,)), dma((2, strips)), dma((2, strips)),
        ],
        compiler_params=pltpu.CompilerParams(
            collective_id=0, has_side_effects=True, vmem_limit_bytes=64 * 2**20
        ),
        cost_estimate=pl.CostEstimate(flops=start.size * 400, bytes_accessed=start.size * 12, transcendentals=0),
    )(start, regions, resistivity)
    return result[None]


def solution(mesh):
    in_specs = (P("tm", "space", None, None), P("space", None, None), P())
    out_specs = P("tm", "space", None, None)
    return jax.shard_map(
        functools.partial(per_device, mesh.shape["tm"], mesh.shape["space"]),
        mesh=mesh, in_specs=in_specs, out_specs=out_specs, check_vma=False,
    )
```

```python
import functools

import jax
import jax.numpy as jnp
from jax import lax
from jax.experimental import pallas as pl
from jax.experimental.pallas import tpu as pltpu
from jax.sharding import PartitionSpec as P

STEPS = 8
fine_step = 0.008
WIDTH = 4
PAD = 8
CHUNK = 128
STRIP = 8
LAG = 1
FLIGHT = 3
HELD = 0
MESH = pl.DeviceIdType.MESH


def coefficient(field, scaled):
    denominator = 1.0 + field * field
    estimate = pl.reciprocal(denominator, approx=True)
    inverse = estimate * (2.0 - denominator * estimate)
    return scaled * (2.0 - inverse)


def sweep(field_at, coeff_at, low, number, row, count, emit):
    rows = pl.ds(row, count)
    lane = lax.broadcasted_iota(jnp.int32, (count, field_at.shape[-1]), 1)
    lanes = field_at.shape[-1]
    is_first, is_last = lane == 0, lane == lanes - 1
    before, here = field_at[low - 1, rows, :], field_at[low, rows, :]
    k_before, k_here = coeff_at[low - 1, rows, :], coeff_at[low, rows, :]
    flux_before = (k_before + k_here) * (here - before)
    held = []
    for position in range(number):
        plane = low + position
        after, k_after = field_at[plane + 1, rows, :], coeff_at[plane + 1, rows, :]
        flux = (k_here + k_after) * (after - here)
        total = flux - flux_before
        for shift in (-1, 1):
            near = pl.ds(row + shift, count)
            total += (k_here + coeff_at[plane, near, :]) * (field_at[plane, near, :] - here)
        right = jnp.where(is_last, 0.0, pltpu.roll(here, lanes - 1, 1))
        k_right = jnp.where(is_last, 0.0, pltpu.roll(k_here, lanes - 1, 1))
        across = (k_here + k_right) * (right - here)
        total += across - jnp.where(is_first, k_here * here, pltpu.roll(across, 1, 1))
        held.append(emit(position, here, total))
        if len(held) > HELD:
            held.pop(0)()
        here, k_here, flux_before = after, k_after, flux
    for store in held:
        store()


def kernel(
    slices, blocks, start_hbm, regions_hbm, resistivity_hbm, out,
    start, regions, resistivity, field_even, field_odd, coeff_even, coeff_odd,
    scaled, halo, outgoing, guess, relay, relay_coeff, input_sem,
    halo_send, halo_recv, scaled_send, scaled_recv, relay_send, relay_recv, rim_send, rim_recv,
):
    count, height, lanes = start.shape
    field, coeff = (field_even, field_odd), (coeff_even, coeff_odd)
    inputs = [
        pltpu.make_async_copy(source, target, input_sem.at[index])
        for index, (source, target) in enumerate(
            ((resistivity_hbm, resistivity), (regions_hbm, regions), (start_hbm, start))
        )
    ]
    for copy in inputs:
        copy.start()
    low, high = WIDTH, WIDTH + count
    me_t, me_s = lax.axis_index("tm"), lax.axis_index("space")
    has_low, has_high = me_s > 0, me_s < blocks - 1
    has_prev, has_next = me_t > 0, me_t < slices - 1
    below, above = (me_t, me_s - 1), (me_t, me_s + 1)
    previous, following = (me_t - 1, me_s), (me_t + 1, me_s)
    sides = ((0, has_low, below), (1, has_high, above))

    def chunks(body, size=CHUNK):
        def turn(index, _):
            body(pl.multiple_of(index * size, size))
            return 0

        lax.fori_loop(0, height // size, turn, 0)

    barrier = pltpu.get_barrier_semaphore()
    partners = [(has_low, below), (has_high, above), (has_prev, previous), (has_next, following)]
    for in_time, step in ((has_prev, -1), (has_next, 1)):
        for present, move in ((has_low, -1), (has_high, 1)):
            partners.append((jnp.logical_and(in_time, present), (me_t + step, me_s + move)))
    for present, target in partners:
        @pl.when(present)
        def _():
            pl.semaphore_signal(barrier, inc=1, device_id=target, device_id_type=MESH)
    for buffer in (*field, *coeff, relay, relay_coeff):
        edge = jnp.zeros((buffer.shape[0], PAD, lanes), jnp.float32)
        buffer[:, pl.ds(0, PAD), :] = edge
        buffer[:, pl.ds(PAD + height, PAD), :] = edge
    for side, present, _ in sides:
        @pl.when(jnp.logical_not(present))
        def _():
            halo[:, side] = jnp.zeros((2, WIDTH, height, lanes), jnp.float32)
            scaled[pl.ds(high * side, WIDTH)] = jnp.zeros((WIDTH, height, lanes), jnp.float32)
            relay[(count + 1) * side, pl.ds(PAD, height), :] = jnp.zeros((height, lanes), jnp.float32)

    pl.semaphore_wait(barrier, sum(jnp.where(present, 1, 0) for present, _ in partners))

    def remote(source, target, send_sem, recv_sem, device):
        return pltpu.make_async_remote_copy(
            src_ref=source, dst_ref=target, send_sem=send_sem, recv_sem=recv_sem,
            device_id=device, device_id_type=MESH,
        )

    def halo_copy(side, device, slot, source):
        return remote(
            source.at[pl.ds((count - WIDTH) * side, WIDTH)], halo.at[slot, 1 - side],
            halo_send.at[slot, side], halo_recv.at[slot, 1 - side], device,
        )

    def scaled_copy(side, device):
        return remote(
            scaled.at[pl.ds(low + (count - WIDTH) * side, WIDTH)],
            scaled.at[pl.ds(high * (1 - side), WIDTH)],
            scaled_send.at[side], scaled_recv.at[1 - side], device,
        )

    for side, present, device in sides:
        @pl.when(present)
        def _():
            halo_copy(side, device, 0, start_hbm).start()

    def lookup(plane, rows):
        region = regions[plane, rows, :]
        value = jnp.zeros(region.shape, jnp.float32)
        for index in range(resistivity.shape[0]):
            value = jnp.where(region == index, resistivity[index] * (0.5 * fine_step), value)
        return value

    order = list(range(WIDTH)) + list(range(count - WIDTH, count))

    def outer_scaled(row):
        for plane in order:
            scaled[low + plane, pl.ds(row, CHUNK), :] = lookup(plane, pl.ds(row, CHUNK))

    inputs[0].wait()
    inputs[1].wait()
    chunks(outer_scaled)
    for side, present, device in sides:
        @pl.when(present)
        def _():
            scaled_copy(side, device).start()

    def prepare(row):
        rows, padded = pl.ds(row, CHUNK), pl.ds(row + PAD, CHUNK)
        for plane in range(count):
            value = start[plane, rows, :]
            if plane in order:
                factor = scaled[low + plane, rows, :]
            else:
                factor = lookup(plane, rows)
                scaled[low + plane, rows, :] = factor
            field_even[low + plane, padded, :] = value
            coeff_even[low + plane, padded, :] = coefficient(value, factor)

    inputs[2].wait()
    chunks(prepare)

    coarse = jnp.float32(STEPS)
    subtract = jnp.where(has_prev, 1.0, 0.0).astype(jnp.float32)

    def fine(turn, inside, first, number, reach=0, side=None, present=None):
        if number <= 0:
            return
        now, later = inside % 2, 1 - inside % 2
        last = inside == WIDTH - 1

        def body(row):
            rows, padded = pl.ds(row, CHUNK), pl.ds(row + PAD, CHUNK)

            def emit(position, value, increment):
                plane = first + position
                stepped = value + increment
                if reach:
                    beyond = jnp.where(side == 0, position < reach, position > inside)
                    grid = jnp.logical_or(present, jnp.logical_not(beyond))
                    stepped = stepped * jnp.where(grid, 1.0, 0.0).astype(jnp.float32)
                factor = coefficient(stepped, scaled[plane, rows, :])
                if inside == 0:
                    ahead = subtract * (value + coarse * increment)
                    ahead = jnp.where(turn == 0, ahead, guess[plane, rows, :])
                if last:
                    result = stepped - guess[plane, rows, :]

                def store():
                    if inside == 0:
                        guess[plane, rows, :] = ahead
                    if last:
                        out[plane - low, rows, :] = result
                        outgoing[plane - low, rows, :] = stepped
                    field[later][plane, padded, :] = stepped
                    coeff[later][plane, padded, :] = factor

                return store

            sweep(field[now], coeff[now], first, number, row + PAD, CHUNK, emit)

        chunks(body)

    rounds = STEPS // WIDTH
    is_even = lax.rem(me_s, 2) == 0

    def one_round(turn, _):
        slot = lax.rem(turn, 2)
        for inside in range(WIDTH):
            fine(turn, inside, low + inside + 1, count - 2 * inside - 2)

        def finish_side(index, _):
            side = jnp.where(is_even, 1 - index, index)
            present = jnp.where(side == 0, has_low, has_high)
            device = (me_t, me_s + 2 * side - 1)

            @pl.when(present)
            def _():
                halo_copy(side, device, slot, outgoing).wait_send()
                halo_copy(1 - side, device, slot, outgoing).wait_recv()

            @pl.when(jnp.logical_and(present, turn == 0))
            def _():
                scaled_copy(side, device).wait_send()
                scaled_copy(1 - side, device).wait_recv()

            def place(row):
                rows, padded = pl.ds(row, CHUNK), pl.ds(row + PAD, CHUNK)
                for plane in range(WIDTH):
                    at = high * side + plane
                    value = halo[slot, side, plane, rows, :]
                    field_even[at, padded, :] = value
                    coeff_even[at, padded, :] = coefficient(value, scaled[at, rows, :])

            chunks(place)
            for inside in range(WIDTH):
                reach = WIDTH - 1 - inside
                first = jnp.where(side == 0, low - reach, high - inside - 1)
                fine(turn, inside, first, WIDTH, reach, side, present)

            @pl.when(jnp.logical_and(present, turn < rounds - 1))
            def _():
                halo_copy(side, device, 1 - slot, outgoing).start()

            return 0

        lax.fori_loop(0, 2, finish_side, 0)
        return 0

    lax.fori_loop(0, rounds, one_round, 0)

    strips = height // STRIP

    def strip_rows(strip, offset):
        return pl.ds(pl.multiple_of(strip * STRIP + offset, STRIP if offset % STRIP == 0 else 8), STRIP)

    def relay_copy(strip, device):
        return remote(
            out.at[:, strip_rows(strip, 0), :],
            relay.at[pl.ds(1, count), strip_rows(strip, PAD), :],
            relay_send.at[strip], relay_recv.at[strip], device,
        )

    def rim_copy(side, strip, device):
        rows = strip_rows(strip, PAD)
        return remote(
            out.at[(count - 1) * side, strip_rows(strip, 0), :],
            relay.at[(count + 1) * (1 - side), rows, :],
            rim_send.at[side, strip], rim_recv.at[1 - side, strip], device,
        )

    def send_strip(strip):
        for side, present, device in sides:
            @pl.when(present)
            def _():
                rim_copy(side, strip, (device[0] + 1, device[1])).start()
        relay_copy(strip, following).start()

    def finish_strip(strip):
        for side, present, device in sides:
            @pl.when(present)
            def _():
                rim_copy(side, strip, (device[0] + 1, device[1])).wait_send()
        relay_copy(strip, following).wait_send()

    @pl.when(jnp.logical_not(has_prev))
    def _():
        for strip in range(FLIGHT):
            send_strip(strip)

        def send(strip, _):
            finish_strip(strip - FLIGHT)
            send_strip(strip)
            return 0

        lax.fori_loop(FLIGHT, strips, send, 0)
        for strip in range(strips - FLIGHT, strips):
            finish_strip(strip)

    @pl.when(has_prev)
    def _():
        def arrive(strip):
            relay_copy(strip, previous).wait_recv()
            rows, padded = strip_rows(strip, 0), strip_rows(strip, PAD)
            for plane in range(count):
                relay_coeff[1 + plane, padded, :] = coefficient(
                    relay[1 + plane, padded, :], scaled[low + plane, rows, :]
                )

        def advance(strip):
            rows, padded = strip_rows(strip, 0), strip_rows(strip, PAD)
            for side, present, device in sides:
                @pl.when(present)
                def _():
                    rim_copy(1 - side, strip, device).wait_recv()
                at = (count + 1) * side
                relay_coeff[at, padded, :] = coefficient(
                    relay[at, padded, :], scaled[low - 1 + at, rows, :]
                )

            def emit(plane, value, increment):
                result = out[plane, rows, :] + (value + coarse * increment)

                def store():
                    out[plane, rows, :] = result

                return store

            sweep(relay, relay_coeff, 1, count, padded.start, STRIP, emit)

            @pl.when(has_next)
            def _():
                send_strip(strip)

        for strip in range(LAG):
            arrive(strip)

        def turn(strip, _):
            arrive(strip)
            advance(strip - LAG)
            return 0

        lax.fori_loop(LAG, strips, turn, 0)
        for strip in range(strips - LAG, strips):
            advance(strip)

    @pl.when(jnp.logical_and(has_prev, has_next))
    def _():
        def finish(strip, _):
            finish_strip(strip)
            return 0

        lax.fori_loop(0, strips, finish, 0)


def per_device(slices, blocks, start_values, regions, resistivity):
    start = start_values[0]
    count, height, lanes = start.shape
    tall, deep = height + 2 * PAD, count + 2 * WIDTH
    strips = height // STRIP
    dma, vmem = pltpu.SemaphoreType.DMA, pltpu.VMEM
    f32 = jnp.float32
    result = pl.pallas_call(
        functools.partial(kernel, slices, blocks),
        out_shape=jax.ShapeDtypeStruct(start.shape, f32),
        in_specs=[
            pl.BlockSpec(memory_space=pltpu.HBM),
            pl.BlockSpec(memory_space=pltpu.HBM),
            pl.BlockSpec(memory_space=pltpu.HBM),
        ],
        out_specs=pl.BlockSpec(memory_space=pltpu.VMEM),
        scratch_shapes=[
            vmem(start.shape, f32),
            vmem(regions.shape, regions.dtype),
            pltpu.SMEM(resistivity.shape, f32),
            *[vmem((deep, tall, lanes), f32) for _ in range(4)],
            vmem((deep, height, lanes), f32),
            vmem((2, 2, WIDTH, height, lanes), f32),
            vmem(start.shape, f32),
            vmem((deep, height, lanes), f32),
            vmem((count + 2, tall, lanes), f32),
            vmem((count + 2, tall, lanes), f32),
            dma((3,)), dma((2, 2)), dma((2, 2)), dma((2,)), dma((2,)),
            dma((strips,)), dma((strips,)), dma((2, strips)), dma((2, strips)),
        ],
        compiler_params=pltpu.CompilerParams(
            collective_id=0, has_side_effects=True, vmem_limit_bytes=64 * 2**20
        ),
        cost_estimate=pl.CostEstimate(flops=start.size * 400, bytes_accessed=start.size * 12, transcendentals=0),
    )(start, regions, resistivity)
    return result[None]


def solution(mesh):
    in_specs = (P("tm", "space", None, None), P("space", None, None), P())
    out_specs = P("tm", "space", None, None)
    return jax.shard_map(
        functools.partial(per_device, mesh.shape["tm"], mesh.shape["space"]),
        mesh=mesh, in_specs=in_specs, out_specs=out_specs, check_vma=False,
    )
```

```python
import functools

import jax
import jax.numpy as jnp
from jax import lax
from jax.experimental import pallas as pl
from jax.experimental.pallas import tpu as pltpu
from jax.sharding import PartitionSpec as P

STEPS = 8
fine_step = 0.008
WIDTH = 4
PAD = 8
CHUNK = 128
STRIP = 8
LAG = 1
FLIGHT = 3
MESH = pl.DeviceIdType.MESH


def coefficient(field, scaled):
    denominator = 1.0 + field * field
    estimate = pl.reciprocal(denominator, approx=True)
    inverse = estimate * (2.0 - denominator * estimate)
    return scaled * (2.0 - inverse)


def sweep(field_at, coeff_at, low, number, row, count, emit, hold):
    rows = pl.ds(row, count)
    lane = lax.broadcasted_iota(jnp.int32, (count, field_at.shape[-1]), 1)
    lanes = field_at.shape[-1]
    is_first, is_last = lane == 0, lane == lanes - 1
    before, here = field_at[low - 1, rows, :], field_at[low, rows, :]
    k_before, k_here = coeff_at[low - 1, rows, :], coeff_at[low, rows, :]
    flux_before = (k_before + k_here) * (here - before)
    held = []
    for position in range(number):
        plane = low + position
        after, k_after = field_at[plane + 1, rows, :], coeff_at[plane + 1, rows, :]
        flux = (k_here + k_after) * (after - here)
        total = flux - flux_before
        for shift in (-1, 1):
            near = pl.ds(row + shift, count)
            total += (k_here + coeff_at[plane, near, :]) * (field_at[plane, near, :] - here)
        right = jnp.where(is_last, 0.0, pltpu.roll(here, lanes - 1, 1))
        k_right = jnp.where(is_last, 0.0, pltpu.roll(k_here, lanes - 1, 1))
        across = (k_here + k_right) * (right - here)
        total += across - jnp.where(is_first, k_here * here, pltpu.roll(across, 1, 1))
        held.append(emit(position, here, total))
        if len(held) > hold:
            held.pop(0)()
        here, k_here, flux_before = after, k_after, flux
    for store in held:
        store()


def kernel(
    slices, blocks, start_hbm, regions_hbm, resistivity_hbm, out,
    start, regions, resistivity, field_even, field_odd, coeff_even, coeff_odd,
    scaled, halo, outgoing, guess, relay, relay_coeff, input_sem,
    halo_send, halo_recv, scaled_send, scaled_recv, relay_send, relay_recv, rim_send, rim_recv,
):
    count, height, lanes = start.shape
    field, coeff = (field_even, field_odd), (coeff_even, coeff_odd)
    inputs = [
        pltpu.make_async_copy(source, target, input_sem.at[index])
        for index, (source, target) in enumerate(
            ((resistivity_hbm, resistivity), (regions_hbm, regions), (start_hbm, start))
        )
    ]
    for copy in inputs:
        copy.start()
    low, high = WIDTH, WIDTH + count
    me_t, me_s = lax.axis_index("tm"), lax.axis_index("space")
    has_low, has_high = me_s > 0, me_s < blocks - 1
    has_prev, has_next = me_t > 0, me_t < slices - 1
    below, above = (me_t, me_s - 1), (me_t, me_s + 1)
    previous, following = (me_t - 1, me_s), (me_t + 1, me_s)
    sides = ((0, has_low, below), (1, has_high, above))

    def chunks(body, size=CHUNK):
        def turn(index, _):
            body(pl.multiple_of(index * size, size))
            return 0

        lax.fori_loop(0, height // size, turn, 0)

    barrier = pltpu.get_barrier_semaphore()
    partners = [(has_low, below), (has_high, above), (has_prev, previous), (has_next, following)]
    for in_time, step in ((has_prev, -1), (has_next, 1)):
        for present, move in ((has_low, -1), (has_high, 1)):
            partners.append((jnp.logical_and(in_time, present), (me_t + step, me_s + move)))
    for present, target in partners:
        @pl.when(present)
        def _():
            pl.semaphore_signal(barrier, inc=1, device_id=target, device_id_type=MESH)
    for buffer in (*field, *coeff, relay, relay_coeff):
        edge = jnp.zeros((buffer.shape[0], PAD, lanes), jnp.float32)
        buffer[:, pl.ds(0, PAD), :] = edge
        buffer[:, pl.ds(PAD + height, PAD), :] = edge
    for side, present, _ in sides:
        @pl.when(jnp.logical_not(present))
        def _():
            halo[:, side] = jnp.zeros((2, WIDTH, height, lanes), jnp.float32)
            scaled[pl.ds(high * side, WIDTH)] = jnp.zeros((WIDTH, height, lanes), jnp.float32)
            relay[(count + 1) * side, pl.ds(PAD, height), :] = jnp.zeros((height, lanes), jnp.float32)

    pl.semaphore_wait(barrier, sum(jnp.where(present, 1, 0) for present, _ in partners))

    def remote(source, target, send_sem, recv_sem, device):
        return pltpu.make_async_remote_copy(
            src_ref=source, dst_ref=target, send_sem=send_sem, recv_sem=recv_sem,
            device_id=device, device_id_type=MESH,
        )

    def halo_copy(side, device, slot, source):
        return remote(
            source.at[pl.ds((count - WIDTH) * side, WIDTH)], halo.at[slot, 1 - side],
            halo_send.at[slot, side], halo_recv.at[slot, 1 - side], device,
        )

    def scaled_copy(side, device):
        return remote(
            scaled.at[pl.ds(low + (count - WIDTH) * side, WIDTH)],
            scaled.at[pl.ds(high * (1 - side), WIDTH)],
            scaled_send.at[side], scaled_recv.at[1 - side], device,
        )

    for side, present, device in sides:
        @pl.when(present)
        def _():
            halo_copy(side, device, 0, start_hbm).start()

    def lookup(plane, rows):
        region = regions[plane, rows, :]
        value = jnp.zeros(region.shape, jnp.float32)
        for index in range(resistivity.shape[0]):
            value = jnp.where(region == index, resistivity[index] * (0.5 * fine_step), value)
        return value

    order = list(range(WIDTH)) + list(range(count - WIDTH, count))

    def outer_scaled(row):
        for plane in order:
            scaled[low + plane, pl.ds(row, CHUNK), :] = lookup(plane, pl.ds(row, CHUNK))

    inputs[0].wait()
    inputs[1].wait()
    chunks(outer_scaled)
    for side, present, device in sides:
        @pl.when(present)
        def _():
            scaled_copy(side, device).start()

    def prepare(row):
        rows, padded = pl.ds(row, CHUNK), pl.ds(row + PAD, CHUNK)
        for plane in range(count):
            value = start[plane, rows, :]
            if plane in order:
                factor = scaled[low + plane, rows, :]
            else:
                factor = lookup(plane, rows)
                scaled[low + plane, rows, :] = factor
            field_even[low + plane, padded, :] = value
            coeff_even[low + plane, padded, :] = coefficient(value, factor)

    inputs[2].wait()
    chunks(prepare)

    coarse = jnp.float32(STEPS)
    subtract = jnp.where(has_prev, 1.0, 0.0).astype(jnp.float32)

    def fine(turn, inside, first, number, reach=0, side=None, present=None):
        if number <= 0:
            return
        now, later = inside % 2, 1 - inside % 2
        last = inside == WIDTH - 1

        def body(row):
            rows, padded = pl.ds(row, CHUNK), pl.ds(row + PAD, CHUNK)

            def emit(position, value, increment):
                plane = first + position
                stepped = value + increment
                if reach:
                    beyond = jnp.where(side == 0, position < reach, position > inside)
                    grid = jnp.logical_or(present, jnp.logical_not(beyond))
                    stepped = stepped * jnp.where(grid, 1.0, 0.0).astype(jnp.float32)
                factor = coefficient(stepped, scaled[plane, rows, :])
                if inside == 0:
                    ahead = subtract * (value + coarse * increment)
                    ahead = jnp.where(turn == 0, ahead, guess[plane, rows, :])
                if last:
                    result = stepped - guess[plane, rows, :]

                def store():
                    if inside == 0:
                        guess[plane, rows, :] = ahead
                    if last:
                        out[plane - low, rows, :] = result
                        outgoing[plane - low, rows, :] = stepped
                    field[later][plane, padded, :] = stepped
                    coeff[later][plane, padded, :] = factor

                return store

            sweep(field[now], coeff[now], first, number, row + PAD, CHUNK, emit, 0)

        chunks(body)

    rounds = STEPS // WIDTH
    is_even = lax.rem(me_s, 2) == 0

    def one_round(turn, _):
        slot = lax.rem(turn, 2)
        for inside in range(WIDTH):
            fine(turn, inside, low + inside + 1, count - 2 * inside - 2)

        def finish_side(index, _):
            side = jnp.where(is_even, 1 - index, index)
            present = jnp.where(side == 0, has_low, has_high)
            device = (me_t, me_s + 2 * side - 1)

            @pl.when(present)
            def _():
                halo_copy(side, device, slot, outgoing).wait_send()
                halo_copy(1 - side, device, slot, outgoing).wait_recv()

            @pl.when(jnp.logical_and(present, turn == 0))
            def _():
                scaled_copy(side, device).wait_send()
                scaled_copy(1 - side, device).wait_recv()

            def place(row):
                rows, padded = pl.ds(row, CHUNK), pl.ds(row + PAD, CHUNK)
                for plane in range(WIDTH):
                    at = high * side + plane
                    value = halo[slot, side, plane, rows, :]
                    field_even[at, padded, :] = value
                    coeff_even[at, padded, :] = coefficient(value, scaled[at, rows, :])

            chunks(place)
            for inside in range(WIDTH):
                reach = WIDTH - 1 - inside
                first = jnp.where(side == 0, low - reach, high - inside - 1)
                fine(turn, inside, first, WIDTH, reach, side, present)

            @pl.when(jnp.logical_and(present, turn < rounds - 1))
            def _():
                halo_copy(side, device, 1 - slot, outgoing).start()

            return 0

        lax.fori_loop(0, 2, finish_side, 0)
        return 0

    lax.fori_loop(0, rounds, one_round, 0)

    strips = height // STRIP

    def strip_rows(strip, offset):
        return pl.ds(pl.multiple_of(strip * STRIP + offset, STRIP if offset % STRIP == 0 else 8), STRIP)

    def relay_copy(strip, device):
        return remote(
            out.at[:, strip_rows(strip, 0), :],
            relay.at[pl.ds(1, count), strip_rows(strip, PAD), :],
            relay_send.at[strip], relay_recv.at[strip], device,
        )

    def rim_copy(side, strip, device):
        rows = strip_rows(strip, PAD)
        return remote(
            out.at[(count - 1) * side, strip_rows(strip, 0), :],
            relay.at[(count + 1) * (1 - side), rows, :],
            rim_send.at[side, strip], rim_recv.at[1 - side, strip], device,
        )

    def send_strip(strip):
        for side, present, device in sides:
            @pl.when(present)
            def _():
                rim_copy(side, strip, (device[0] + 1, device[1])).start()
        relay_copy(strip, following).start()

    def finish_strip(strip):
        for side, present, device in sides:
            @pl.when(present)
            def _():
                rim_copy(side, strip, (device[0] + 1, device[1])).wait_send()
        relay_copy(strip, following).wait_send()

    @pl.when(jnp.logical_not(has_prev))
    def _():
        for strip in range(FLIGHT):
            send_strip(strip)

        def send(strip, _):
            finish_strip(strip - FLIGHT)
            send_strip(strip)
            return 0

        lax.fori_loop(FLIGHT, strips, send, 0)
        for strip in range(strips - FLIGHT, strips):
            finish_strip(strip)

    @pl.when(has_prev)
    def _():
        def arrive(strip):
            relay_copy(strip, previous).wait_recv()
            rows, padded = strip_rows(strip, 0), strip_rows(strip, PAD)
            for plane in range(count):
                relay_coeff[1 + plane, padded, :] = coefficient(
                    relay[1 + plane, padded, :], scaled[low + plane, rows, :]
                )

        def advance(strip):
            rows, padded = strip_rows(strip, 0), strip_rows(strip, PAD)
            for side, present, device in sides:
                @pl.when(present)
                def _():
                    rim_copy(1 - side, strip, device).wait_recv()
                at = (count + 1) * side
                relay_coeff[at, padded, :] = coefficient(
                    relay[at, padded, :], scaled[low - 1 + at, rows, :]
                )

            def emit(plane, value, increment):
                result = out[plane, rows, :] + (value + coarse * increment)

                def store():
                    out[plane, rows, :] = result

                return store

            sweep(relay, relay_coeff, 1, count, padded.start, STRIP, emit, count)

            @pl.when(has_next)
            def _():
                send_strip(strip)

        for strip in range(LAG):
            arrive(strip)

        def turn(strip, _):
            arrive(strip)
            advance(strip - LAG)
            return 0

        lax.fori_loop(LAG, strips, turn, 0)
        for strip in range(strips - LAG, strips):
            advance(strip)

    @pl.when(jnp.logical_and(has_prev, has_next))
    def _():
        def finish(strip, _):
            finish_strip(strip)
            return 0

        lax.fori_loop(0, strips, finish, 0)


def per_device(slices, blocks, start_values, regions, resistivity):
    start = start_values[0]
    count, height, lanes = start.shape
    tall, deep = height + 2 * PAD, count + 2 * WIDTH
    strips = height // STRIP
    dma, vmem = pltpu.SemaphoreType.DMA, pltpu.VMEM
    f32 = jnp.float32
    result = pl.pallas_call(
        functools.partial(kernel, slices, blocks),
        out_shape=jax.ShapeDtypeStruct(start.shape, f32),
        in_specs=[
            pl.BlockSpec(memory_space=pltpu.HBM),
            pl.BlockSpec(memory_space=pltpu.HBM),
            pl.BlockSpec(memory_space=pltpu.HBM),
        ],
        out_specs=pl.BlockSpec(memory_space=pltpu.VMEM),
        scratch_shapes=[
            vmem(start.shape, f32),
            vmem(regions.shape, regions.dtype),
            pltpu.SMEM(resistivity.shape, f32),
            *[vmem((deep, tall, lanes), f32) for _ in range(4)],
            vmem((deep, height, lanes), f32),
            vmem((2, 2, WIDTH, height, lanes), f32),
            vmem(start.shape, f32),
            vmem((deep, height, lanes), f32),
            vmem((count + 2, tall, lanes), f32),
            vmem((count + 2, tall, lanes), f32),
            dma((3,)), dma((2, 2)), dma((2, 2)), dma((2,)), dma((2,)),
            dma((strips,)), dma((strips,)), dma((2, strips)), dma((2, strips)),
        ],
        compiler_params=pltpu.CompilerParams(
            collective_id=0, has_side_effects=True, vmem_limit_bytes=64 * 2**20
        ),
        cost_estimate=pl.CostEstimate(flops=start.size * 400, bytes_accessed=start.size * 12, transcendentals=0),
    )(start, regions, resistivity)
    return result[None]


def solution(mesh):
    in_specs = (P("tm", "space", None, None), P("space", None, None), P())
    out_specs = P("tm", "space", None, None)
    return jax.shard_map(
        functools.partial(per_device, mesh.shape["tm"], mesh.shape["space"]),
        mesh=mesh, in_specs=in_specs, out_specs=out_specs, check_vma=False,
    )
```
